32 devices in a mesh: groups: 2 (over y), frames: 4 (over z), fsdp: 2 (over x), heads: 2 (over core).
Axes of the slice: x: 2, y: 2, z: 4, core: 2. Of those that a mesh axis runs over, the one named last changes fastest.
Arguments:
- frames_in: bfloat16 [4, 768, 1536], P(('groups', 'fsdp'), 'frames', 'heads'), parts along dimension 0, may hold values from -6 to 6
- lengths: int32 [4], P(('groups', 'fsdp')), parts along dimension 0, may hold values from 192 to 768, as said below
- w_query: bfloat16 [1536, 768], P(('frames', 'fsdp'), 'heads')
- w_key: bfloat16 [1536, 768], P(('frames', 'fsdp'), 'heads'), may hold values from -0.15625 to 0.15625
- w_value: bfloat16 [1536, 768], P(('frames', 'fsdp'), 'heads'), may hold values from -0.15625 to 0.15625
- w_out: bfloat16 [768, 1536], P('heads', ('frames', 'fsdp')), may hold values from -0.21875 to 0.21875
- w_glu: bfloat16 [1536, 2, 1536], P('fsdp', None, 'heads'), may hold values from -0.15625 to 0.15625
- dw_kernel: bfloat16 [31, 1536], P(None, 'heads'), may hold values from -1 to 1
- w_pw: bfloat16 [1536, 1536], P('heads', 'fsdp'), may hold values from -0.15625 to 0.15625
Outputs:
- block_out: bfloat16 [4, 768, 1536], P(('groups', 'fsdp'), 'frames', 'heads'), parts along dimension 0
The draws below stay inside these ranges and needn't reach their ends.
There are 2 independent parts, one for each index of `groups`. The reference program is written for one: setup_inputs(seed, part) draws one part's arguments, and reference() takes and returns one part's arrays. A program takes and returns all parts, laid end to end along the dimension named above; an argument that names none is the same for every part. Nothing has to cross between parts.
Inputs may be any that keep to these rules, and one draw needn't show every extreme that they name: `lengths`: each utterance counts at least 192 valid frames, and in every group some utterance is valid over all 768 frames.
All inputs are finite; a program needn't handle non-finite values.
Results may differ from the reference program's by a relative error of at most 0.012.
The reference program's roundings to bfloat16 on the way (of `normed`, `queries`, `probs`, `context`, `stream`, `normed_two`, `gated` and `hidden`) count: a program that leaves them out, or rounds other values in their place, can miss the bound.
Values may be sent and summed in bfloat16 or wider, within the bound.
A program may use at most 64 MiB of HBM per device.

```python
import math
import jax
import jax.numpy as jnp
from jax import lax

D = 1536
HEAD_DIM = 96
KERNEL = 31
HEADS = 8
UTTS = 2
LEN = 768
D_ATT = 768


def draw_lengths(key, part):
    drawn = jax.random.randint(key, (UTTS,), LEN // 4, LEN + 1, dtype=jnp.int32)
    chosen = jax.random.randint(jax.random.fold_in(key, 1), (), 0, UTTS, dtype=jnp.int32)
    return jnp.where(jnp.arange(UTTS, dtype=jnp.int32) == chosen, LEN, drawn).astype(jnp.int32)


def draw_w_query(key, part):
    base_scale = 2.0 / math.sqrt(D)
    entries = jnp.clip(jax.random.normal(key, (D, D_ATT), jnp.float32), -6.0, 6.0)
    return (entries * base_scale).astype(jnp.bfloat16)


def shard_levels(rng, dims, split, smallest, top_value):
    def one(axis_at, parts):
        draws = jax.random.uniform(jax.random.fold_in(jax.random.fold_in(rng, 6), axis_at), (parts,), jnp.float32, smallest / len(split), top_value / len(split))
        return jnp.repeat(jnp.exp(draws), dims[axis_at] // parts).reshape((-1,) + (1,) * (len(dims) - axis_at - 1))

    factor_of = one(*split[0])
    for cut in split[1:]:
        factor_of = factor_of * one(*cut)
    return factor_of


def gaussian(own_key, extent, width, bound, cuts=(), kind=jnp.bfloat16):
    values = jax.random.normal(own_key, extent, jnp.float32) * width
    if len(cuts) > 0:
        values = shard_levels(own_key, extent, cuts, -0.22, 0.18) * values
    return jnp.clip(values, min=-bound, max=bound).astype(kind)


def setup_inputs(seed: int = 0, part: int = 0) -> dict:
    seeds = jax.random.split(jax.random.key(seed), 10)
    part_splits = jax.random.split(jax.random.fold_in(seeds[9], part), 10)
    frames_in = gaussian(part_splits[0], (UTTS, LEN, D), 1.0, 6.0, ((0, 2), (1, 4), (2, 2)))
    lengths = draw_lengths(jax.random.fold_in(jax.random.fold_in(seeds[9], part), 71), part)
    w_query = draw_w_query(jax.random.fold_in(seeds[9], 71), part)
    w_key = gaussian(seeds[3], (D, D_ATT), D ** -0.5, 0.15625, ((0, 8), (1, 2)))
    w_value = gaussian(seeds[4], (D, D_ATT), D ** -0.5, 0.15625, ((0, 8), (1, 2)))
    w_out = gaussian(seeds[5], (D_ATT, D), D_ATT ** -0.5, 0.21875, ((0, 2), (1, 8)))
    w_glu = gaussian(seeds[6], (D, 2, D), D ** -0.5, 0.15625, ((0, 2), (2, 2)))
    dw_kernel = gaussian(seeds[7], (KERNEL, D), KERNEL ** -0.5, 1.0, ((1, 2),))
    w_pw = gaussian(seeds[8], (D, D), D ** -0.5, 0.15625, ((0, 2), (1, 2)))
    return {"frames_in": frames_in, "lengths": lengths, "w_query": w_query, "w_key": w_key, "w_value": w_value, "w_out": w_out, "w_glu": w_glu, "dw_kernel": dw_kernel, "w_pw": w_pw}


EPS = 1e-05
NEG_FILL = -1e+30

def layer_norm(rows):
    values = rows.astype(jnp.float32)
    mean_row = lax.optimization_barrier(jnp.mean(values, axis=-1, keepdims=True))
    centred = values - mean_row
    variance = lax.optimization_barrier(jnp.mean(centred * centred, axis=-1, keepdims=True))
    return centred * lax.rsqrt(variance + EPS)

def reference(frames_in, lengths, w_query, w_key, w_value, w_out, w_glu, dw_kernel, w_pw):
    scale_factor = 1.0 / math.sqrt(HEAD_DIM)

    def one_utterance(packed):
        rows, length = packed
        normed = layer_norm(rows).astype(jnp.bfloat16)
        queries = jnp.dot(normed, w_query, preferred_element_type=jnp.float32).astype(jnp.bfloat16)
        key_rows = jnp.dot(normed, w_key, preferred_element_type=jnp.float32).astype(jnp.bfloat16)
        value_rows = jnp.dot(normed, w_value, preferred_element_type=jnp.float32).astype(jnp.bfloat16)
        positions = jnp.arange(LEN, dtype=jnp.int32)
        valid = positions < length

        def one_head(head_args):
            query_head, key_head, value_head = head_args
            scores = jnp.dot(query_head, key_head.T, preferred_element_type=jnp.float32) * scale_factor
            masked = jnp.where(valid[None, :], scores, NEG_FILL)
            row_max = lax.optimization_barrier(jnp.max(masked, axis=1, keepdims=True))
            expo = jnp.where(valid[None, :], jnp.exp(scores - row_max), 0.0)
            denom = lax.optimization_barrier(jnp.sum(expo, axis=1, keepdims=True))
            probs = expo.astype(jnp.bfloat16)
            return jnp.dot(probs, value_head, preferred_element_type=jnp.float32) / denom

        def by_head(matrix):
            return matrix.reshape(LEN, HEADS, HEAD_DIM).transpose(1, 0, 2)
        context = lax.map(one_head, (by_head(queries), by_head(key_rows), by_head(value_rows)))
        context = context.transpose(1, 0, 2).reshape(LEN, D_ATT).astype(jnp.bfloat16)
        stream = (rows.astype(jnp.float32) + jnp.dot(context, w_out, preferred_element_type=jnp.float32)).astype(jnp.bfloat16)
        normed_two = layer_norm(stream).astype(jnp.bfloat16)
        projected = jnp.dot(normed_two, w_glu.reshape(D, 2 * D), preferred_element_type=jnp.float32).reshape(LEN, 2, D)
        gated = projected[:, 0, :] * jax.nn.sigmoid(projected[:, 1, :])
        gated = jnp.where(valid[:, None], gated, 0.0).astype(jnp.bfloat16)
        rim = KERNEL // 2
        padded = jnp.pad(gated.astype(jnp.float32), ((rim, rim), (0, 0)))
        depth = jnp.zeros((LEN, D), jnp.float32)
        for tap_index in range(KERNEL):
            depth = depth + padded[tap_index:tap_index + LEN] * dw_kernel[tap_index].astype(jnp.float32)
        hidden = (depth * jax.nn.sigmoid(depth)).astype(jnp.bfloat16)
        conv_term = jnp.dot(hidden, w_pw, preferred_element_type=jnp.float32)
        return (stream.astype(jnp.float32) + conv_term).astype(jnp.bfloat16)
    return lax.map(one_utterance, (frames_in, lengths))
```

```python
import functools
import math

import jax
import jax.numpy as jnp
from jax import lax
from jax.experimental import pallas as pl
from jax.experimental.pallas import tpu as pltpu
from jax.sharding import PartitionSpec as P

HEAD_DIM = 96
KERNEL = 31


EPS = 1e-05
NEG_FILL = -1e30


def padded_2(cells, sides, width):
    for axis, dim in sides:
        count = lax.axis_size(axis)
        ends = count - 1
        head = lax.slice_in_dim(cells, 0, width, axis=dim)
        tail = lax.slice_in_dim(cells, cells.shape[dim] - width, cells.shape[dim], axis=dim)
        cells = jnp.concatenate(
            [
                lax.ppermute(tail, axis, [(i, (i + 1) % count) for i in range(ends)]),
                cells,
                lax.ppermute(head, axis, [((i + 1) % count, i) for i in range(ends)]),
            ],
            axis=dim,
        )
    return cells


def layer_norm(rows):
    values = rows.astype(jnp.float32)
    mean_row = jnp.mean(values, axis=-1, keepdims=True)
    centred = values - mean_row
    variance = jnp.mean(centred * centred, axis=-1, keepdims=True)
    return centred * lax.rsqrt(variance + EPS)


def shards(frames_in, lengths, w_query, w_key, w_value, w_out, w_glu, dw_kernel, w_pw):
    full_rows = lax.all_gather(frames_in, "heads", axis=2, tiled=True)[0]
    frame_count = full_rows.shape[0]
    half_width = frames_in.shape[2]
    own_start = lax.axis_index("heads") * half_width
    normed = layer_norm(full_rows).astype(jnp.bfloat16)
    att_cols = w_query.shape[1]
    pieces = (
        lax.all_gather(w_query, ("frames", "fsdp"), axis=0, tiled=True),
        lax.all_gather(w_key, ("frames", "fsdp"), axis=0, tiled=True),
        lax.all_gather(w_value, ("frames", "fsdp"), axis=0, tiled=True),
    )
    sliced = normed
    projected = tuple(
        (jnp.dot(sliced, piece_part, preferred_element_type=jnp.float32) for piece_part in pieces)
    )
    head_count = att_cols // HEAD_DIM
    queries = projected[0].astype(jnp.bfloat16).reshape(frame_count, head_count, HEAD_DIM)
    key_rows = projected[1].astype(jnp.bfloat16)
    value_rows = projected[2].astype(jnp.bfloat16)
    length = lengths[0]
    scale_factor = 1.0 / math.sqrt(HEAD_DIM)
    start_max = jnp.full((frame_count, head_count), NEG_FILL, jnp.float32)
    pieces = (
        lax.all_gather(key_rows, "frames", axis=0, tiled=True),
        lax.all_gather(value_rows, "frames", axis=0, tiled=True),
    )
    key_block = pieces[0].reshape(-1, head_count, HEAD_DIM)
    value_block = pieces[1].reshape(-1, head_count, HEAD_DIM)
    block_rows = key_block.shape[0]
    scores = (
        jnp.einsum("qhd,khd->qhk", queries, key_block, preferred_element_type=jnp.float32)
        * scale_factor
    )
    valid = jnp.arange(block_rows, dtype=jnp.int32) < length
    masked = jnp.where(valid, scores, NEG_FILL)
    new_max = jnp.maximum(start_max, jnp.max(masked, axis=2))
    expo = jnp.where(valid, jnp.exp(masked - new_max[:, :, None]), 0.0)
    new_sum = jnp.sum(expo, axis=2)
    block_acc = jnp.einsum(
        "qhk,khd->qhd", expo.astype(jnp.bfloat16), value_block, preferred_element_type=jnp.float32
    )
    context = (block_acc / new_sum[:, :, None]).reshape(frame_count, att_cols).astype(jnp.bfloat16)
    partial_value = jnp.dot(
        context,
        lax.all_gather(w_out, ("frames", "fsdp"), axis=1, tiled=True),
        preferred_element_type=jnp.float32,
    )
    total = lax.psum(partial_value.astype(jnp.bfloat16), "heads").astype(jnp.float32)
    stream_full = (full_rows.astype(jnp.float32) + total).astype(jnp.bfloat16)
    stream_own = lax.dynamic_slice_in_dim(stream_full, own_start, half_width, 1)
    normed_two = layer_norm(stream_full).astype(jnp.bfloat16)
    channels = w_glu.shape[2]
    sliced = normed_two
    glu_pre = jnp.einsum(
        "td,dgc->tgc",
        sliced,
        lax.all_gather(w_glu, "fsdp", axis=0, tiled=True),
        preferred_element_type=jnp.float32,
    )
    positions = lax.axis_index("frames") * frame_count + jnp.arange(frame_count, dtype=jnp.int32)
    live = positions < length
    gated = jnp.where(
        live[:, None], glu_pre[:, 0, :] * jax.nn.sigmoid(glu_pre[:, 1, :]), 0.0
    ).astype(jnp.bfloat16)
    padded = padded_2(gated, (("frames", 0),), KERNEL // 2)
    depth = jnp.zeros((frame_count, channels), jnp.float32)
    for tap_index in range(KERNEL):
        depth = depth + padded[tap_index : tap_index + frame_count].astype(jnp.float32) * dw_kernel[
            tap_index
        ].astype(jnp.float32)
    hidden = (depth * jax.nn.sigmoid(depth)).astype(jnp.bfloat16)
    conv_part = jnp.dot(
        hidden, lax.all_gather(w_pw, "fsdp", axis=1, tiled=True), preferred_element_type=jnp.float32
    )
    conv_half = lax.psum_scatter(
        conv_part.astype(jnp.bfloat16), "heads", scatter_dimension=1, tiled=True
    ).astype(jnp.float32)
    result = (stream_own.astype(jnp.float32) + conv_half).astype(jnp.bfloat16)
    return result[None]


MESH = pl.DeviceIdType.MESH
HALO = 16


def block_kernel(
    frames_ref, length_ref, shard_ref, glu_ref, taps_ref, pw_ref, out_ref,
    full, packed, glu_all, pw_all, normed, qkv, kv_all, context,
    part, part_in, stream, padded, edge, edge_in, hidden, conv, conv_in,
    local_sem, send_sem, recv_sem,
):
    rows, half = frames_ref.shape
    width = 2 * half
    shard_rows = shard_ref.shape[0]
    att = shard_ref.shape[1] // 4
    g, f = lax.axis_index("groups"), lax.axis_index("frames")
    s, h = lax.axis_index("fsdp"), lax.axis_index("heads")
    ring = lax.axis_size("frames")
    right, left = lax.rem(f + 1, ring), lax.rem(f + ring - 1, ring)
    across = lax.rem(f + 2, ring)
    peers = {
        "right": {"frames": right}, "left": {"frames": left},
        "x": {"fsdp": 1 - s}, "y": {"groups": 1 - g}, "core": {"heads": 1 - h},
    }
    names = {}

    def copy(name, src, dst, to):
        slot = names.setdefault(name, len(names))
        return pltpu.make_async_remote_copy(
            src_ref=src, dst_ref=dst, send_sem=send_sem.at[slot], recv_sem=recv_sem.at[slot],
            device_id=peers[to], device_id_type=MESH,
        )

    barrier = pltpu.get_barrier_semaphore()
    for to in peers:
        pl.semaphore_signal(barrier, inc=1, device_id=peers[to], device_id_type=MESH)
    pl.semaphore_wait(barrier, len(peers))

    started = []

    def start(c):
        c.start()
        started.append(c)
        return c

    def rows_at(index, first=0, count=shard_rows):
        return pl.ds(pl.multiple_of(index * shard_rows + first, 16), count)

    mid = shard_rows // 2
    own_half = g * mid
    columns = {"qkv": pl.ds(0, 3 * att), "out": pl.ds(3 * att, att)}

    def at(kind, place, axis_s, first=0, count=shard_rows):
        return packed.at[rows_at(place * 2 + axis_s, first, count), columns[kind]]

    def own_src(kind, first=0, count=shard_rows):
        return shard_ref.at[pl.ds(pl.multiple_of(first, 16), count), columns[kind]]

    swap = start(copy("frames", frames_ref, full.at[h], "core"))
    z_copies, x_copies, y_copies = {}, {}, {}

    def z_first(kind):
        for to in ("right", "left"):
            z_copies[kind, to, 0] = start(
                copy((kind, to, 0), own_src(kind), at(kind, f, s), to)
            )

    def x_send(kind, place_name, place):
        src = own_src(kind, own_half, mid) if place_name == "own" else at(kind, place, s, own_half, mid)
        x_copies[kind, place_name] = start(
            copy((kind, "x", place_name), src, at(kind, place, s, own_half, mid), "x")
        )

    def y_forward(kind, place_name, place):
        x_copies[kind, place_name].wait_recv()
        block = at(kind, place, 1 - s, own_half, mid)
        y_copies[kind, place_name] = start(copy((kind, "y", place_name), block, block, "y"))

    def z_second(kind):
        z_copies[kind, "right", 0].wait_recv()
        top = at(kind, left, s, 0, mid)
        z_copies[kind, "right", 1] = start(copy((kind, "right", 1), top, top, "right"))
        x_send(kind, "left", left)
        z_copies[kind, "left", 0].wait_recv()
        low = at(kind, right, s, mid, mid)
        z_copies[kind, "left", 1] = start(copy((kind, "left", 1), low, low, "left"))
        x_send(kind, "right", right)

    def z_last(kind):
        z_copies[kind, "right", 1].wait_recv()
        z_copies[kind, "left", 1].wait_recv()
        x_send(kind, "across", across)

    places = {"own": f, "left": left, "right": right, "across": across}

    glu_rows = glu_ref.shape[0]
    glu_part = glu_rows // 4
    pw_rows = pw_ref.shape[0]
    pw_part = pw_rows // 2
    wide = {}

    def glu_block(axis_s, piece):
        return glu_all.at[axis_s, pl.ds(pl.multiple_of((g * 2 + piece) * glu_part, 16), glu_part), :]

    def glu_send(piece):
        src = glu_ref.at[pl.ds(pl.multiple_of((g * 2 + piece) * glu_part, 16), glu_part), :]
        wide["glu", "x", piece] = start(copy(("glu", "x", piece), src, glu_block(s, piece), "x"))

    def glu_forward(piece):
        wide["glu", "x", piece].wait_recv()
        block = glu_block(1 - s, piece)
        wide["glu", "y", piece] = start(copy(("glu", "y", piece), block, block, "y"))

    def pw_block(axis_s):
        return pw_all.at[axis_s, pl.ds(pl.multiple_of(g * pw_part, 16), pw_part), :]

    def pw_send():
        src = pw_ref.at[pl.ds(pl.multiple_of(g * pw_part, 16), pw_part), :]
        wide["pw", "x"] = start(copy(("pw", "x"), src, pw_block(s), "x"))

    def pw_forward():
        wide["pw", "x"].wait_recv()
        block = pw_block(1 - s)
        wide["pw", "y"] = start(copy(("pw", "y"), block, block, "y"))

    def layer(read):
        lo, hi = read(0), read(1)
        mean = (jnp.sum(lo, axis=1, keepdims=True) + jnp.sum(hi, axis=1, keepdims=True)) / width
        lo, hi = lo - mean, hi - mean
        var = (jnp.sum(lo * lo, axis=1, keepdims=True) + jnp.sum(hi * hi, axis=1, keepdims=True)) / width
        scale = lax.rsqrt(var + EPS)
        normed[:, :half] = (lo * scale).astype(jnp.bfloat16)
        normed[:, half:] = (hi * scale).astype(jnp.bfloat16)

    z_first("qkv")
    x_send("qkv", "own", f)
    here = [
        pltpu.make_async_copy(frames_ref, full.at[h], local_sem.at[0]),
        pltpu.make_async_copy(shard_ref, packed.at[rows_at(f * 2 + s), :], local_sem.at[1]),
        pltpu.make_async_copy(glu_ref, glu_all.at[s], local_sem.at[2]),
        pltpu.make_async_copy(pw_ref, pw_all.at[s], local_sem.at[3]),
    ]
    for c in here:
        c.start()
    here[0].wait()
    swap.wait_recv()
    layer(lambda i: full[i].astype(jnp.float32))
    y_forward("qkv", "own", f)
    z_second("qkv")
    z_first("out")
    y_forward("qkv", "left", left)
    y_forward("qkv", "right", right)
    z_last("qkv")
    glu_send(0)
    y_forward("qkv", "across", across)
    x_send("out", "own", f)
    glu_send(1)
    here[1].wait()
    for name in places:
        y_copies["qkv", name].wait_recv()

    def project(tile):
        cols = pl.ds(tile * att, att)
        qkv[tile] = jnp.dot(
            normed[...], packed[:, cols], preferred_element_type=jnp.float32
        ).astype(jnp.bfloat16)

    project(1)
    project(2)

    def kv_rows(place, first=0, count=rows):
        return pl.ds(pl.multiple_of(place * rows + first, 16), count)

    kv_all[0, kv_rows(f), :] = qkv[1]
    kv_all[1, kv_rows(f), :] = qkv[2]
    own_kv = kv_all.at[:, kv_rows(f), :]
    kv = [start(copy(("kv", to), own_kv, own_kv, to)) for to in ("right", "left")]
    project(0)
    y_or = rows // 2
    kv[0].wait_recv()
    block = kv_all.at[:, kv_rows(left, 0, y_or), :]
    kv.append(start(copy(("kv", "right", 1), block, block, "right")))
    kv[1].wait_recv()
    block = kv_all.at[:, kv_rows(right, y_or, y_or), :]
    kv.append(start(copy(("kv", "left", 1), block, block, "left")))
    z_second("out")
    y_forward("out", "own", f)
    glu_forward(0)
    glu_forward(1)
    z_last("out")
    y_forward("out", "left", left)
    y_forward("out", "right", right)
    y_forward("out", "across", across)
    pw_send()
    kv[2].wait_recv()
    kv[3].wait_recv()

    length = length_ref[0]
    total = kv_all.shape[1]
    valid = lax.broadcasted_iota(jnp.int32, (1, total), 1) < length
    column = lax.broadcasted_iota(jnp.int32, (1, att), 1)
    scale_factor = 1.0 / math.sqrt(HEAD_DIM)
    gathered = jnp.zeros((rows, att), jnp.float32)
    for head in range(att // HEAD_DIM):
        mine = (column >= head * HEAD_DIM) & (column < (head + 1) * HEAD_DIM)
        query = jnp.where(mine, qkv[0].astype(jnp.float32), 0.0).astype(jnp.bfloat16)
        scores = lax.dot_general(
            query, kv_all[0], (((1,), (1,)), ((), ())), preferred_element_type=jnp.float32
        ) * scale_factor
        masked = jnp.where(valid, scores, NEG_FILL)
        top = jnp.max(masked, axis=1, keepdims=True)
        expo = jnp.where(valid, jnp.exp(masked - top), 0.0)
        denom = jnp.sum(expo, axis=1, keepdims=True)
        mixed = jnp.dot(
            expo.astype(jnp.bfloat16), kv_all[1], preferred_element_type=jnp.float32
        )
        gathered = jnp.where(mine, mixed / denom, gathered)
    context[...] = gathered.astype(jnp.bfloat16)

    for name in places:
        y_copies["out", name].wait_recv()
    for i in range(2):
        part[i] = lax.dot_general(
            context[...], packed[i * half : (i + 1) * half, 3 * att :],
            (((1,), (1,)), ((), ())), preferred_element_type=jnp.float32,
        ).astype(jnp.bfloat16)
    summed = start(copy("part", part, part_in, "core"))
    pw_forward()
    summed.wait_recv()
    for i in range(2):
        both = (part[i].astype(jnp.float32) + part_in[i].astype(jnp.float32)).astype(jnp.bfloat16)
        stream[i] = (full[i].astype(jnp.float32) + both.astype(jnp.float32)).astype(jnp.bfloat16)
    layer(lambda i: stream[i].astype(jnp.float32))

    here[2].wait()
    wide["glu", "y", 0].wait_recv()
    wide["glu", "y", 1].wait_recv()
    live = f * rows + lax.broadcasted_iota(jnp.int32, (rows, 1), 0) < length
    tile_cols = 256

    @pl.loop(0, half // tile_cols)
    def _(tile):
        first = pl.multiple_of(tile * tile_cols, tile_cols)
        pre = []
        for base in (0, half):
            cols = pl.ds(base + first, tile_cols)
            pre.append(
                jnp.dot(normed[:, :half], glu_all[0, :, cols], preferred_element_type=jnp.float32)
                + jnp.dot(normed[:, half:], glu_all[1, :, cols], preferred_element_type=jnp.float32)
            )
        gated = jnp.where(live, pre[0] * jax.nn.sigmoid(pre[1]), 0.0).astype(jnp.bfloat16)
        cols = pl.ds(first, tile_cols)
        edge[0, :, cols] = gated[:HALO]
        edge[1, :, cols] = gated[rows - HALO :]
        padded[pl.ds(HALO, rows), cols] = gated.astype(jnp.float32)

    tail = start(copy("tail", edge.at[1], edge_in.at[0], "right"))
    head = start(copy("head", edge.at[0], edge_in.at[1], "left"))
    tail.wait_recv()
    head.wait_recv()
    has_left = jnp.where(f > 0, 1.0, 0.0)
    has_right = jnp.where(f < ring - 1, 1.0, 0.0)
    padded[:HALO, :] = edge_in[0].astype(jnp.float32) * has_left
    padded[HALO + rows :, :] = edge_in[1].astype(jnp.float32) * has_right

    lanes = 128
    step_rows = 64

    @pl.loop(0, half // lanes)
    def _(tile):
        cols = pl.ds(pl.multiple_of(tile * lanes, lanes), lanes)
        taps = taps_ref[:, cols].astype(jnp.float32)
        for first in range(0, rows, step_rows):
            depth = jnp.zeros((step_rows, lanes), jnp.float32)
            for tap in range(KERNEL):
                at_row = first + tap + HALO - KERNEL // 2
                depth = depth + padded[at_row : at_row + step_rows, cols] * taps[tap : tap + 1]
            hidden[first : first + step_rows, cols] = (depth * jax.nn.sigmoid(depth)).astype(jnp.bfloat16)

    here[3].wait()
    wide["pw", "y"].wait_recv()
    conv[1] = jnp.dot(
        hidden[...], pw_all[1 - h], preferred_element_type=jnp.float32
    ).astype(jnp.bfloat16)
    given = start(copy("conv", conv.at[1], conv_in, "core"))
    conv[0] = jnp.dot(
        hidden[...], pw_all[h], preferred_element_type=jnp.float32
    ).astype(jnp.bfloat16)
    given.wait_recv()
    both = (conv[0].astype(jnp.float32) + conv_in[...].astype(jnp.float32)).astype(jnp.bfloat16)
    out_ref[...] = (stream[h].astype(jnp.float32) + both.astype(jnp.float32)).astype(jnp.bfloat16)
    for c in started:
        c.wait_send()


def fused(frames_in, lengths, w_query, w_key, w_value, w_out, w_glu, dw_kernel, w_pw):
    rows, half = frames_in.shape[1:]
    att = w_query.shape[1]
    width = 2 * half
    ring = lax.axis_size("frames")
    shard = jnp.concatenate([w_query, w_key, w_value, w_out.T], axis=1)
    glu = w_glu.reshape(w_glu.shape[0], 2 * w_glu.shape[2])
    bf16, f32 = jnp.bfloat16, jnp.float32
    vmem = pl.BlockSpec(memory_space=pltpu.VMEM)
    anywhere = pl.BlockSpec(memory_space=pl.ANY)
    copies = 40
    result = pl.pallas_call(
        block_kernel,
        out_shape=jax.ShapeDtypeStruct((rows, half), bf16),
        in_specs=[anywhere, pl.BlockSpec(memory_space=pltpu.SMEM), anywhere, anywhere, vmem, anywhere],
        out_specs=vmem,
        scratch_shapes=[
            pltpu.VMEM((2, rows, half), bf16),
            pltpu.VMEM((width, 4 * att), bf16),
            pltpu.VMEM((2,) + glu.shape, bf16),
            pltpu.VMEM((2,) + w_pw.shape, bf16),
            pltpu.VMEM((rows, width), bf16),
            pltpu.VMEM((3, rows, att), bf16),
            pltpu.VMEM((2, ring * rows, att), bf16),
            pltpu.VMEM((rows, att), bf16),
            pltpu.VMEM((2, rows, half), bf16),
            pltpu.VMEM((2, rows, half), bf16),
            pltpu.VMEM((2, rows, half), bf16),
            pltpu.VMEM((rows + 2 * HALO, half), f32),
            pltpu.VMEM((2, HALO, half), bf16),
            pltpu.VMEM((2, HALO, half), bf16),
            pltpu.VMEM((rows, half), bf16),
            pltpu.VMEM((2, rows, half), bf16),
            pltpu.VMEM((rows, half), bf16),
            pltpu.SemaphoreType.DMA((4,)),
            pltpu.SemaphoreType.DMA((copies,)),
            pltpu.SemaphoreType.DMA((copies,)),
        ],
        compiler_params=pltpu.CompilerParams(
            collective_id=0, has_side_effects=True, vmem_limit_bytes=52 * 2**20
        ),
        cost_estimate=pl.CostEstimate(
            flops=2 * rows * width * (3 * att + 4 * half), bytes_accessed=2 * width * (4 * att + 6 * half),
            transcendentals=rows * rows * ring * 4,
        ),
    )(frames_in[0], lengths, shard, glu, dw_kernel, w_pw)
    return result[None]


def fits(mesh):
    sizes = dict(mesh.shape)
    return sizes["groups"] == 2 and sizes["fsdp"] == 2 and sizes["heads"] == 2 and sizes["frames"] == 4


def solution(mesh):
    in_specs = (
        P(("groups", "fsdp"), "frames", "heads"),
        P(("groups", "fsdp")),
        P(("frames", "fsdp"), "heads"),
        P(("frames", "fsdp"), "heads"),
        P(("frames", "fsdp"), "heads"),
        P("heads", ("frames", "fsdp")),
        P("fsdp", None, "heads"),
        P(None, "heads"),
        P("heads", "fsdp"),
    )
    out_specs = P(("groups", "fsdp"), "frames", "heads")
    body = fused if fits(mesh) else shards
    return jax.shard_map(body, mesh=mesh, in_specs=in_specs, out_specs=out_specs, check_vma=False)
```

```python
import functools
import math

import jax
import jax.numpy as jnp
from jax import lax
from jax.experimental import pallas as pl
from jax.experimental.pallas import tpu as pltpu
from jax.sharding import PartitionSpec as P

HEAD_DIM = 96
KERNEL = 31


EPS = 1e-05
NEG_FILL = -1e30


def padded_2(cells, sides, width):
    for axis, dim in sides:
        count = lax.axis_size(axis)
        ends = count - 1
        head = lax.slice_in_dim(cells, 0, width, axis=dim)
        tail = lax.slice_in_dim(cells, cells.shape[dim] - width, cells.shape[dim], axis=dim)
        cells = jnp.concatenate(
            [
                lax.ppermute(tail, axis, [(i, (i + 1) % count) for i in range(ends)]),
                cells,
                lax.ppermute(head, axis, [((i + 1) % count, i) for i in range(ends)]),
            ],
            axis=dim,
        )
    return cells


def layer_norm(rows):
    values = rows.astype(jnp.float32)
    mean_row = jnp.mean(values, axis=-1, keepdims=True)
    centred = values - mean_row
    variance = jnp.mean(centred * centred, axis=-1, keepdims=True)
    return centred * lax.rsqrt(variance + EPS)


def shards(frames_in, lengths, w_query, w_key, w_value, w_out, w_glu, dw_kernel, w_pw):
    full_rows = lax.all_gather(frames_in, "heads", axis=2, tiled=True)[0]
    frame_count = full_rows.shape[0]
    half_width = frames_in.shape[2]
    own_start = lax.axis_index("heads") * half_width
    normed = layer_norm(full_rows).astype(jnp.bfloat16)
    att_cols = w_query.shape[1]
    pieces = (
        lax.all_gather(w_query, ("frames", "fsdp"), axis=0, tiled=True),
        lax.all_gather(w_key, ("frames", "fsdp"), axis=0, tiled=True),
        lax.all_gather(w_value, ("frames", "fsdp"), axis=0, tiled=True),
    )
    sliced = normed
    projected = tuple(
        (jnp.dot(sliced, piece_part, preferred_element_type=jnp.float32) for piece_part in pieces)
    )
    head_count = att_cols // HEAD_DIM
    queries = projected[0].astype(jnp.bfloat16).reshape(frame_count, head_count, HEAD_DIM)
    key_rows = projected[1].astype(jnp.bfloat16)
    value_rows = projected[2].astype(jnp.bfloat16)
    length = lengths[0]
    scale_factor = 1.0 / math.sqrt(HEAD_DIM)
    start_max = jnp.full((frame_count, head_count), NEG_FILL, jnp.float32)
    pieces = (
        lax.all_gather(key_rows, "frames", axis=0, tiled=True),
        lax.all_gather(value_rows, "frames", axis=0, tiled=True),
    )
    key_block = pieces[0].reshape(-1, head_count, HEAD_DIM)
    value_block = pieces[1].reshape(-1, head_count, HEAD_DIM)
    block_rows = key_block.shape[0]
    scores = (
        jnp.einsum("qhd,khd->qhk", queries, key_block, preferred_element_type=jnp.float32)
        * scale_factor
    )
    valid = jnp.arange(block_rows, dtype=jnp.int32) < length
    masked = jnp.where(valid, scores, NEG_FILL)
    new_max = jnp.maximum(start_max, jnp.max(masked, axis=2))
    expo = jnp.where(valid, jnp.exp(masked - new_max[:, :, None]), 0.0)
    new_sum = jnp.sum(expo, axis=2)
    block_acc = jnp.einsum(
        "qhk,khd->qhd", expo.astype(jnp.bfloat16), value_block, preferred_element_type=jnp.float32
    )
    context = (block_acc / new_sum[:, :, None]).reshape(frame_count, att_cols).astype(jnp.bfloat16)
    partial_value = jnp.dot(
        context,
        lax.all_gather(w_out, ("frames", "fsdp"), axis=1, tiled=True),
        preferred_element_type=jnp.float32,
    )
    total = lax.psum(partial_value.astype(jnp.bfloat16), "heads").astype(jnp.float32)
    stream_full = (full_rows.astype(jnp.float32) + total).astype(jnp.bfloat16)
    stream_own = lax.dynamic_slice_in_dim(stream_full, own_start, half_width, 1)
    normed_two = layer_norm(stream_full).astype(jnp.bfloat16)
    channels = w_glu.shape[2]
    sliced = normed_two
    glu_pre = jnp.einsum(
        "td,dgc->tgc",
        sliced,
        lax.all_gather(w_glu, "fsdp", axis=0, tiled=True),
        preferred_element_type=jnp.float32,
    )
    positions = lax.axis_index("frames") * frame_count + jnp.arange(frame_count, dtype=jnp.int32)
    live = positions < length
    gated = jnp.where(
        live[:, None], glu_pre[:, 0, :] * jax.nn.sigmoid(glu_pre[:, 1, :]), 0.0
    ).astype(jnp.bfloat16)
    padded = padded_2(gated, (("frames", 0),), KERNEL // 2)
    depth = jnp.zeros((frame_count, channels), jnp.float32)
    for tap_index in range(KERNEL):
        depth = depth + padded[tap_index : tap_index + frame_count].astype(jnp.float32) * dw_kernel[
            tap_index
        ].astype(jnp.float32)
    hidden = (depth * jax.nn.sigmoid(depth)).astype(jnp.bfloat16)
    conv_part = jnp.dot(
        hidden, lax.all_gather(w_pw, "fsdp", axis=1, tiled=True), preferred_element_type=jnp.float32
    )
    conv_half = lax.psum_scatter(
        conv_part.astype(jnp.bfloat16), "heads", scatter_dimension=1, tiled=True
    ).astype(jnp.float32)
    result = (stream_own.astype(jnp.float32) + conv_half).astype(jnp.bfloat16)
    return result[None]


MESH = pl.DeviceIdType.MESH
HALO = 16


def block_kernel(
    frames_ref, length_ref, shard_ref, glu_ref, taps_ref, pw_ref, out_ref,
    full, packed, glu_all, pw_all, normed, qkv, kv_all, context,
    part, part_in, stream, padded, edge, edge_in, hidden, conv, conv_in,
    local_sem, send_sem, recv_sem,
):
    rows, half = frames_ref.shape
    width = 2 * half
    shard_rows = shard_ref.shape[0]
    att = shard_ref.shape[1] // 4
    g, f = lax.axis_index("groups"), lax.axis_index("frames")
    s, h = lax.axis_index("fsdp"), lax.axis_index("heads")
    ring = lax.axis_size("frames")
    right, left = lax.rem(f + 1, ring), lax.rem(f + ring - 1, ring)
    across = lax.rem(f + 2, ring)
    peers = {
        "right": {"frames": right}, "left": {"frames": left},
        "x": {"fsdp": 1 - s}, "y": {"groups": 1 - g}, "core": {"heads": 1 - h},
    }
    names = {}

    def copy(name, src, dst, to):
        slot = names.setdefault(name, len(names))
        return pltpu.make_async_remote_copy(
            src_ref=src, dst_ref=dst, send_sem=send_sem.at[slot], recv_sem=recv_sem.at[slot],
            device_id=peers[to], device_id_type=MESH,
        )

    barrier = pltpu.get_barrier_semaphore()
    for to in peers:
        pl.semaphore_signal(barrier, inc=1, device_id=peers[to], device_id_type=MESH)
    pl.semaphore_wait(barrier, len(peers))

    started = []

    def start(c):
        c.start()
        started.append(c)
        return c

    def rows_at(index, first=0, count=shard_rows):
        return pl.ds(pl.multiple_of(index * shard_rows + first, 16), count)

    mid = shard_rows // 2
    own_half = g * mid
    columns = {"qkv": pl.ds(0, 3 * att), "out": pl.ds(3 * att, att)}

    def at(kind, place, axis_s, first=0, count=shard_rows):
        return packed.at[rows_at(place * 2 + axis_s, first, count), columns[kind]]

    def own_src(kind, first=0, count=shard_rows):
        return shard_ref.at[pl.ds(pl.multiple_of(first, 16), count), columns[kind]]

    def frame_rows(place, first=0, count=rows):
        return pl.ds(pl.multiple_of(place * rows + first, 16), count)

    def frames_at(place, first=0, count=rows):
        return full.at[h, frame_rows(place, first, count), :]

    swaps = {"own": start(copy(("frames", "own"), frames_ref, frames_at(f), "core"))}
    frame_copies = {}

    def frames_first():
        for to in ("right", "left"):
            frame_copies[to, 0] = start(copy(("frames", to, 0), frames_ref, frames_at(f), to))

    def frames_swap(name, place):
        block = frames_at(place)
        swaps[name] = start(copy(("frames", name), block, block, "core"))

    def frames_second():
        frame_mid = rows // 2
        frame_copies["right", 0].wait_recv()
        block = frames_at(left, 0, frame_mid)
        frame_copies["right", 1] = start(copy(("frames", "right", 1), block, block, "right"))
        frames_swap("left", left)
        frame_copies["left", 0].wait_recv()
        block = frames_at(right, frame_mid, frame_mid)
        frame_copies["left", 1] = start(copy(("frames", "left", 1), block, block, "left"))
        frames_swap("right", right)

    def frames_last():
        frame_copies["right", 1].wait_recv()
        frame_copies["left", 1].wait_recv()
        frames_swap("across", across)

    z_copies, x_copies, y_copies = {}, {}, {}

    def z_first(kind):
        for to in ("right", "left"):
            z_copies[kind, to, 0] = start(
                copy((kind, to, 0), own_src(kind), at(kind, f, s), to)
            )

    def x_send(kind, place_name, place):
        src = own_src(kind, own_half, mid) if place_name == "own" else at(kind, place, s, own_half, mid)
        x_copies[kind, place_name] = start(
            copy((kind, "x", place_name), src, at(kind, place, s, own_half, mid), "x")
        )

    def y_forward(kind, place_name, place):
        x_copies[kind, place_name].wait_recv()
        block = at(kind, place, 1 - s, own_half, mid)
        y_copies[kind, place_name] = start(copy((kind, "y", place_name), block, block, "y"))

    def z_second(kind):
        z_copies[kind, "right", 0].wait_recv()
        top = at(kind, left, s, 0, mid)
        z_copies[kind, "right", 1] = start(copy((kind, "right", 1), top, top, "right"))
        x_send(kind, "left", left)
        z_copies[kind, "left", 0].wait_recv()
        low = at(kind, right, s, mid, mid)
        z_copies[kind, "left", 1] = start(copy((kind, "left", 1), low, low, "left"))
        x_send(kind, "right", right)

    def z_last(kind):
        z_copies[kind, "right", 1].wait_recv()
        z_copies[kind, "left", 1].wait_recv()
        x_send(kind, "across", across)

    places = {"own": f, "left": left, "right": right, "across": across}

    glu_rows = glu_ref.shape[0]
    glu_part = glu_rows // 4
    pw_rows = pw_ref.shape[0]
    pw_part = pw_rows // 2
    wide = {}

    def glu_block(axis_s, piece):
        return glu_all.at[axis_s, pl.ds(pl.multiple_of((g * 2 + piece) * glu_part, 16), glu_part), :]

    def glu_send(piece):
        src = glu_ref.at[pl.ds(pl.multiple_of((g * 2 + piece) * glu_part, 16), glu_part), :]
        wide["glu", "x", piece] = start(copy(("glu", "x", piece), src, glu_block(s, piece), "x"))

    def glu_forward(piece):
        wide["glu", "x", piece].wait_recv()
        block = glu_block(1 - s, piece)
        wide["glu", "y", piece] = start(copy(("glu", "y", piece), block, block, "y"))

    def pw_block(axis_s):
        return pw_all.at[axis_s, pl.ds(pl.multiple_of(g * pw_part, 16), pw_part), :]

    def pw_send():
        src = pw_ref.at[pl.ds(pl.multiple_of(g * pw_part, 16), pw_part), :]
        wide["pw", "x"] = start(copy(("pw", "x"), src, pw_block(s), "x"))

    def pw_forward():
        wide["pw", "x"].wait_recv()
        block = pw_block(1 - s)
        wide["pw", "y"] = start(copy(("pw", "y"), block, block, "y"))

    def layer(read, at_rows):
        lo, hi = read(0), read(1)
        mean = (jnp.sum(lo, axis=1, keepdims=True) + jnp.sum(hi, axis=1, keepdims=True)) / width
        lo, hi = lo - mean, hi - mean
        var = (jnp.sum(lo * lo, axis=1, keepdims=True) + jnp.sum(hi * hi, axis=1, keepdims=True)) / width
        scale = lax.rsqrt(var + EPS)
        normed[at_rows, :half] = (lo * scale).astype(jnp.bfloat16)
        normed[at_rows, half:] = (hi * scale).astype(jnp.bfloat16)

    z_first("qkv")
    x_send("qkv", "own", f)
    frames_first()
    glu_send(0)
    here = [
        pltpu.make_async_copy(frames_ref, frames_at(f), local_sem.at[0]),
        pltpu.make_async_copy(shard_ref, packed.at[rows_at(f * 2 + s), :], local_sem.at[1]),
        pltpu.make_async_copy(glu_ref, glu_all.at[s], local_sem.at[2]),
        pltpu.make_async_copy(pw_ref, pw_all.at[s], local_sem.at[3]),
    ]
    for c in here:
        c.start()

    def layer_block(name, place):
        swaps[name].wait_recv()
        where = frame_rows(place)
        layer(lambda i: full[i, where, :].astype(jnp.float32), where)

    here[0].wait()
    layer_block("own", f)
    y_forward("qkv", "own", f)
    z_second("qkv")
    frames_second()
    z_first("out")
    y_forward("qkv", "left", left)
    y_forward("qkv", "right", right)
    glu_forward(0)
    z_last("qkv")
    x_send("out", "own", f)
    glu_send(1)
    layer_block("left", left)
    layer_block("right", right)
    y_forward("qkv", "across", across)
    frames_last()
    y_forward("out", "own", f)
    layer_block("across", across)
    here[1].wait()
    for name in places:
        y_copies["qkv", name].wait_recv()

    @pl.loop(0, ring)
    def _(place):
        where = frame_rows(place)
        for i in range(2):
            kv_all[i, where, :] = jnp.dot(
                normed[where, :], packed[:, (i + 1) * att : (i + 2) * att],
                preferred_element_type=jnp.float32,
            ).astype(jnp.bfloat16)

    z_second("out")
    pw_send()
    qkv[...] = jnp.dot(
        normed[frame_rows(f), :], packed[:, :att], preferred_element_type=jnp.float32
    ).astype(jnp.bfloat16)
    glu_forward(1)

    y_forward("out", "left", left)
    y_forward("out", "right", right)
    z_last("out")

    length = length_ref[0]
    total = kv_all.shape[1]
    valid = lax.broadcasted_iota(jnp.int32, (1, total), 1) < length
    column = lax.broadcasted_iota(jnp.int32, (1, att), 1)
    scale_factor = 1.0 / math.sqrt(HEAD_DIM)
    gathered = jnp.zeros((rows, att), jnp.float32)
    for head in range(att // HEAD_DIM):
        mine = (column >= head * HEAD_DIM) & (column < (head + 1) * HEAD_DIM)
        query = jnp.where(mine, qkv[...].astype(jnp.float32), 0.0).astype(jnp.bfloat16)
        scores = lax.dot_general(
            query, kv_all[0], (((1,), (1,)), ((), ())), preferred_element_type=jnp.float32
        ) * scale_factor
        masked = jnp.where(valid, scores, NEG_FILL)
        top = jnp.max(masked, axis=1, keepdims=True)
        expo = jnp.where(valid, jnp.exp(masked - top), 0.0)
        denom = jnp.sum(expo, axis=1, keepdims=True)
        mixed = jnp.dot(
            expo.astype(jnp.bfloat16), kv_all[1], preferred_element_type=jnp.float32
        )
        gathered = jnp.where(mine, mixed / denom, gathered)
    context[...] = gathered.astype(jnp.bfloat16)

    y_forward("out", "across", across)
    pw_forward()
    for name in places:
        y_copies["out", name].wait_recv()
    for i in range(2):
        part[i] = lax.dot_general(
            context[...], packed[i * half : (i + 1) * half, 3 * att :],
            (((1,), (1,)), ((), ())), preferred_element_type=jnp.float32,
        ).astype(jnp.bfloat16)
    summed = start(copy("part", part, part_in, "core"))
    summed.wait_recv()
    for i in range(2):
        both = (part[i].astype(jnp.float32) + part_in[i].astype(jnp.float32)).astype(jnp.bfloat16)
        stream[i] = (full[i, frame_rows(f), :].astype(jnp.float32) + both.astype(jnp.float32)).astype(jnp.bfloat16)
    layer(lambda i: stream[i].astype(jnp.float32), pl.ds(0, rows))

    here[2].wait()
    wide["glu", "y", 0].wait_recv()
    wide["glu", "y", 1].wait_recv()
    live = f * rows + lax.broadcasted_iota(jnp.int32, (rows, 1), 0) < length
    tile_cols = 256

    @pl.loop(0, half // tile_cols)
    def _(tile):
        first = pl.multiple_of(tile * tile_cols, tile_cols)
        pre = []
        for base in (0, half):
            cols = pl.ds(base + first, tile_cols)
            pre.append(
                jnp.dot(normed[:rows, :half], glu_all[0, :, cols], preferred_element_type=jnp.float32)
                + jnp.dot(normed[:rows, half:], glu_all[1, :, cols], preferred_element_type=jnp.float32)
            )
        gated = jnp.where(live, pre[0] * jax.nn.sigmoid(pre[1]), 0.0).astype(jnp.bfloat16)
        cols = pl.ds(first, tile_cols)
        edge[0, :, cols] = gated[:HALO]
        edge[1, :, cols] = gated[rows - HALO :]
        padded[pl.ds(HALO, rows), cols] = gated.astype(jnp.float32)

    tail = start(copy("tail", edge.at[1], edge_in.at[0], "right"))
    head = start(copy("head", edge.at[0], edge_in.at[1], "left"))
    tail.wait_recv()
    head.wait_recv()
    has_left = jnp.where(f > 0, 1.0, 0.0)
    has_right = jnp.where(f < ring - 1, 1.0, 0.0)
    padded[:HALO, :] = edge_in[0].astype(jnp.float32) * has_left
    padded[HALO + rows :, :] = edge_in[1].astype(jnp.float32) * has_right

    lanes = 128
    step_rows = 64

    @pl.loop(0, half // lanes)
    def _(tile):
        cols = pl.ds(pl.multiple_of(tile * lanes, lanes), lanes)
        taps = taps_ref[:, cols].astype(jnp.float32)
        for first in range(0, rows, step_rows):
            depth = jnp.zeros((step_rows, lanes), jnp.float32)
            for tap in range(KERNEL):
                at_row = first + tap + HALO - KERNEL // 2
                depth = depth + padded[at_row : at_row + step_rows, cols] * taps[tap : tap + 1]
            hidden[first : first + step_rows, cols] = (depth * jax.nn.sigmoid(depth)).astype(jnp.bfloat16)

    here[3].wait()
    wide["pw", "y"].wait_recv()
    conv[1] = jnp.dot(
        hidden[...], pw_all[1 - h], preferred_element_type=jnp.float32
    ).astype(jnp.bfloat16)
    given = start(copy("conv", conv.at[1], conv_in, "core"))
    conv[0] = jnp.dot(
        hidden[...], pw_all[h], preferred_element_type=jnp.float32
    ).astype(jnp.bfloat16)
    given.wait_recv()
    both = (conv[0].astype(jnp.float32) + conv_in[...].astype(jnp.float32)).astype(jnp.bfloat16)
    out_ref[...] = (stream[h].astype(jnp.float32) + both.astype(jnp.float32)).astype(jnp.bfloat16)
    for c in started:
        c.wait_send()


def fused(frames_in, lengths, w_query, w_key, w_value, w_out, w_glu, dw_kernel, w_pw):
    rows, half = frames_in.shape[1:]
    att = w_query.shape[1]
    width = 2 * half
    ring = lax.axis_size("frames")
    shard = jnp.concatenate([w_query, w_key, w_value, w_out.T], axis=1)
    glu = w_glu.reshape(w_glu.shape[0], 2 * w_glu.shape[2])
    bf16, f32 = jnp.bfloat16, jnp.float32
    vmem = pl.BlockSpec(memory_space=pltpu.VMEM)
    anywhere = pl.BlockSpec(memory_space=pl.ANY)
    copies = 48
    result = pl.pallas_call(
        block_kernel,
        out_shape=jax.ShapeDtypeStruct((rows, half), bf16),
        in_specs=[anywhere, pl.BlockSpec(memory_space=pltpu.SMEM), anywhere, anywhere, vmem, anywhere],
        out_specs=vmem,
        scratch_shapes=[
            pltpu.VMEM((2, ring * rows, half), bf16),
            pltpu.VMEM((width, 4 * att), bf16),
            pltpu.VMEM((2,) + glu.shape, bf16),
            pltpu.VMEM((2,) + w_pw.shape, bf16),
            pltpu.VMEM((ring * rows, width), bf16),
            pltpu.VMEM((rows, att), bf16),
            pltpu.VMEM((2, ring * rows, att), bf16),
            pltpu.VMEM((rows, att), bf16),
            pltpu.VMEM((2, rows, half), bf16),
            pltpu.VMEM((2, rows, half), bf16),
            pltpu.VMEM((2, rows, half), bf16),
            pltpu.VMEM((rows + 2 * HALO, half), f32),
            pltpu.VMEM((2, HALO, half), bf16),
            pltpu.VMEM((2, HALO, half), bf16),
            pltpu.VMEM((rows, half), bf16),
            pltpu.VMEM((2, rows, half), bf16),
            pltpu.VMEM((rows, half), bf16),
            pltpu.SemaphoreType.DMA((4,)),
            pltpu.SemaphoreType.DMA((copies,)),
            pltpu.SemaphoreType.DMA((copies,)),
        ],
        compiler_params=pltpu.CompilerParams(
            collective_id=0, has_side_effects=True, vmem_limit_bytes=52 * 2**20
        ),
        cost_estimate=pl.CostEstimate(
            flops=2 * rows * width * (3 * att + 4 * half), bytes_accessed=2 * width * (4 * att + 6 * half),
            transcendentals=rows * rows * ring * 4,
        ),
    )(frames_in[0], lengths, shard, glu, dw_kernel, w_pw)
    return result[None]


def fits(mesh):
    sizes = dict(mesh.shape)
    return sizes["groups"] == 2 and sizes["fsdp"] == 2 and sizes["heads"] == 2 and sizes["frames"] == 4


def solution(mesh):
    in_specs = (
        P(("groups", "fsdp"), "frames", "heads"),
        P(("groups", "fsdp")),
        P(("frames", "fsdp"), "heads"),
        P(("frames", "fsdp"), "heads"),
        P(("frames", "fsdp"), "heads"),
        P("heads", ("frames", "fsdp")),
        P("fsdp", None, "heads"),
        P(None, "heads"),
        P("heads", "fsdp"),
    )
    out_specs = P(("groups", "fsdp"), "frames", "heads")
    body = fused if fits(mesh) else shards
    return jax.shard_map(body, mesh=mesh, in_specs=in_specs, out_specs=out_specs, check_vma=False)
```

```python
import functools
import math

import jax
import jax.numpy as jnp
from jax import lax
from jax.experimental import pallas as pl
from jax.experimental.pallas import tpu as pltpu
from jax.sharding import PartitionSpec as P

HEAD_DIM = 96
KERNEL = 31


EPS = 1e-05
NEG_FILL = -1e30


def padded_2(cells, sides, width):
    for axis, dim in sides:
        count = lax.axis_size(axis)
        ends = count - 1
        head = lax.slice_in_dim(cells, 0, width, axis=dim)
        tail = lax.slice_in_dim(cells, cells.shape[dim] - width, cells.shape[dim], axis=dim)
        cells = jnp.concatenate(
            [
                lax.ppermute(tail, axis, [(i, (i + 1) % count) for i in range(ends)]),
                cells,
                lax.ppermute(head, axis, [((i + 1) % count, i) for i in range(ends)]),
            ],
            axis=dim,
        )
    return cells


def layer_norm(rows):
    values = rows.astype(jnp.float32)
    mean_row = jnp.mean(values, axis=-1, keepdims=True)
    centred = values - mean_row
    variance = jnp.mean(centred * centred, axis=-1, keepdims=True)
    return centred * lax.rsqrt(variance + EPS)


def shards(frames_in, lengths, w_query, w_key, w_value, w_out, w_glu, dw_kernel, w_pw):
    full_rows = lax.all_gather(frames_in, "heads", axis=2, tiled=True)[0]
    frame_count = full_rows.shape[0]
    half_width = frames_in.shape[2]
    own_start = lax.axis_index("heads") * half_width
    normed = layer_norm(full_rows).astype(jnp.bfloat16)
    att_cols = w_query.shape[1]
    pieces = (
        lax.all_gather(w_query, ("frames", "fsdp"), axis=0, tiled=True),
        lax.all_gather(w_key, ("frames", "fsdp"), axis=0, tiled=True),
        lax.all_gather(w_value, ("frames", "fsdp"), axis=0, tiled=True),
    )
    sliced = normed
    projected = tuple(
        (jnp.dot(sliced, piece_part, preferred_element_type=jnp.float32) for piece_part in pieces)
    )
    head_count = att_cols // HEAD_DIM
    queries = projected[0].astype(jnp.bfloat16).reshape(frame_count, head_count, HEAD_DIM)
    key_rows = projected[1].astype(jnp.bfloat16)
    value_rows = projected[2].astype(jnp.bfloat16)
    length = lengths[0]
    scale_factor = 1.0 / math.sqrt(HEAD_DIM)
    start_max = jnp.full((frame_count, head_count), NEG_FILL, jnp.float32)
    pieces = (
        lax.all_gather(key_rows, "frames", axis=0, tiled=True),
        lax.all_gather(value_rows, "frames", axis=0, tiled=True),
    )
    key_block = pieces[0].reshape(-1, head_count, HEAD_DIM)
    value_block = pieces[1].reshape(-1, head_count, HEAD_DIM)
    block_rows = key_block.shape[0]
    scores = (
        jnp.einsum("qhd,khd->qhk", queries, key_block, preferred_element_type=jnp.float32)
        * scale_factor
    )
    valid = jnp.arange(block_rows, dtype=jnp.int32) < length
    masked = jnp.where(valid, scores, NEG_FILL)
    new_max = jnp.maximum(start_max, jnp.max(masked, axis=2))
    expo = jnp.where(valid, jnp.exp(masked - new_max[:, :, None]), 0.0)
    new_sum = jnp.sum(expo, axis=2)
    block_acc = jnp.einsum(
        "qhk,khd->qhd", expo.astype(jnp.bfloat16), value_block, preferred_element_type=jnp.float32
    )
    context = (block_acc / new_sum[:, :, None]).reshape(frame_count, att_cols).astype(jnp.bfloat16)
    partial_value = jnp.dot(
        context,
        lax.all_gather(w_out, ("frames", "fsdp"), axis=1, tiled=True),
        preferred_element_type=jnp.float32,
    )
    total = lax.psum(partial_value.astype(jnp.bfloat16), "heads").astype(jnp.float32)
    stream_full = (full_rows.astype(jnp.float32) + total).astype(jnp.bfloat16)
    stream_own = lax.dynamic_slice_in_dim(stream_full, own_start, half_width, 1)
    normed_two = layer_norm(stream_full).astype(jnp.bfloat16)
    channels = w_glu.shape[2]
    sliced = normed_two
    glu_pre = jnp.einsum(
        "td,dgc->tgc",
        sliced,
        lax.all_gather(w_glu, "fsdp", axis=0, tiled=True),
        preferred_element_type=jnp.float32,
    )
    positions = lax.axis_index("frames") * frame_count + jnp.arange(frame_count, dtype=jnp.int32)
    live = positions < length
    gated = jnp.where(
        live[:, None], glu_pre[:, 0, :] * jax.nn.sigmoid(glu_pre[:, 1, :]), 0.0
    ).astype(jnp.bfloat16)
    padded = padded_2(gated, (("frames", 0),), KERNEL // 2)
    depth = jnp.zeros((frame_count, channels), jnp.float32)
    for tap_index in range(KERNEL):
        depth = depth + padded[tap_index : tap_index + frame_count].astype(jnp.float32) * dw_kernel[
            tap_index
        ].astype(jnp.float32)
    hidden = (depth * jax.nn.sigmoid(depth)).astype(jnp.bfloat16)
    conv_part = jnp.dot(
        hidden, lax.all_gather(w_pw, "fsdp", axis=1, tiled=True), preferred_element_type=jnp.float32
    )
    conv_half = lax.psum_scatter(
        conv_part.astype(jnp.bfloat16), "heads", scatter_dimension=1, tiled=True
    ).astype(jnp.float32)
    result = (stream_own.astype(jnp.float32) + conv_half).astype(jnp.bfloat16)
    return result[None]


MESH = pl.DeviceIdType.MESH
HALO = 16


def block_kernel(
    frames_ref, length_ref, shard_ref, glu_ref, taps_ref, pw_ref, out_ref,
    full, packed, glu_all, pw_all, normed, qkv, kv_all, context,
    part, part_in, stream, padded, edge, edge_in, hidden, conv, conv_in,
    local_sem, send_sem, recv_sem,
):
    rows, half = frames_ref.shape
    width = 2 * half
    shard_rows = shard_ref.shape[0]
    att = shard_ref.shape[1] // 4
    g, f = lax.axis_index("groups"), lax.axis_index("frames")
    s, h = lax.axis_index("fsdp"), lax.axis_index("heads")
    ring = lax.axis_size("frames")
    right, left = lax.rem(f + 1, ring), lax.rem(f + ring - 1, ring)
    across = lax.rem(f + 2, ring)
    peers = {
        "right": {"frames": right}, "left": {"frames": left},
        "x": {"fsdp": 1 - s}, "y": {"groups": 1 - g}, "core": {"heads": 1 - h},
    }
    names = {}

    def copy(name, src, dst, to):
        slot = names.setdefault(name, len(names))
        return pltpu.make_async_remote_copy(
            src_ref=src, dst_ref=dst, send_sem=send_sem.at[slot], recv_sem=recv_sem.at[slot],
            device_id=peers[to], device_id_type=MESH,
        )

    barrier = pltpu.get_barrier_semaphore()
    for to in peers:
        pl.semaphore_signal(barrier, inc=1, device_id=peers[to], device_id_type=MESH)
    pl.semaphore_wait(barrier, len(peers))

    started = []

    def start(c):
        c.start()
        started.append(c)
        return c

    def rows_at(index, first=0, count=shard_rows):
        return pl.ds(pl.multiple_of(index * shard_rows + first, 16), count)

    mid = shard_rows // 2
    own_half = g * mid
    columns = {"qkv": pl.ds(0, 3 * att), "out": pl.ds(3 * att, att)}

    def at(kind, place, axis_s, first=0, count=shard_rows):
        return packed.at[rows_at(place * 2 + axis_s, first, count), columns[kind]]

    def own_src(kind, first=0, count=shard_rows):
        return shard_ref.at[pl.ds(pl.multiple_of(first, 16), count), columns[kind]]

    def frame_rows(place, first=0, count=rows):
        return pl.ds(pl.multiple_of(place * rows + first, 16), count)

    def frames_at(place, first=0, count=rows):
        return full.at[h, frame_rows(place, first, count), :]

    swaps = {"own": start(copy(("frames", "own"), frames_ref, frames_at(f), "core"))}
    frame_copies = {}

    def frames_first():
        for to in ("right", "left"):
            frame_copies[to, 0] = start(copy(("frames", to, 0), frames_ref, frames_at(f), to))

    def frames_swap(name, place):
        block = frames_at(place)
        swaps[name] = start(copy(("frames", name), block, block, "core"))

    def frames_second():
        frame_mid = rows // 2
        frame_copies["right", 0].wait_recv()
        block = frames_at(left, 0, frame_mid)
        frame_copies["right", 1] = start(copy(("frames", "right", 1), block, block, "right"))
        frames_swap("left", left)
        frame_copies["left", 0].wait_recv()
        block = frames_at(right, frame_mid, frame_mid)
        frame_copies["left", 1] = start(copy(("frames", "left", 1), block, block, "left"))
        frames_swap("right", right)

    def frames_last():
        frame_copies["right", 1].wait_recv()
        frame_copies["left", 1].wait_recv()
        frames_swap("across", across)

    z_copies, x_copies, y_copies = {}, {}, {}

    def z_first(kind):
        for to in ("right", "left"):
            z_copies[kind, to, 0] = start(
                copy((kind, to, 0), own_src(kind), at(kind, f, s), to)
            )

    def x_send(kind, place_name, place):
        src = own_src(kind, own_half, mid) if place_name == "own" else at(kind, place, s, own_half, mid)
        x_copies[kind, place_name] = start(
            copy((kind, "x", place_name), src, at(kind, place, s, own_half, mid), "x")
        )

    def y_forward(kind, place_name, place):
        x_copies[kind, place_name].wait_recv()
        block = at(kind, place, 1 - s, own_half, mid)
        y_copies[kind, place_name] = start(copy((kind, "y", place_name), block, block, "y"))

    def z_second(kind):
        z_copies[kind, "right", 0].wait_recv()
        top = at(kind, left, s, 0, mid)
        z_copies[kind, "right", 1] = start(copy((kind, "right", 1), top, top, "right"))
        x_send(kind, "left", left)
        z_copies[kind, "left", 0].wait_recv()
        low = at(kind, right, s, mid, mid)
        z_copies[kind, "left", 1] = start(copy((kind, "left", 1), low, low, "left"))
        x_send(kind, "right", right)

    def z_last(kind):
        z_copies[kind, "right", 1].wait_recv()
        z_copies[kind, "left", 1].wait_recv()
        x_send(kind, "across", across)

    places = {"own": f, "left": left, "right": right, "across": across}

    glu_rows = glu_ref.shape[0]
    glu_part = glu_rows // 4
    pw_rows = pw_ref.shape[0]
    pw_part = pw_rows // 4
    wide = {}

    def glu_block(axis_s, piece):
        return glu_all.at[axis_s, pl.ds(pl.multiple_of((g * 2 + piece) * glu_part, 16), glu_part), :]

    def glu_send(piece):
        src = glu_ref.at[pl.ds(pl.multiple_of((g * 2 + piece) * glu_part, 16), glu_part), :]
        wide["glu", "x", piece] = start(copy(("glu", "x", piece), src, glu_block(s, piece), "x"))

    def glu_forward(piece):
        wide["glu", "x", piece].wait_recv()
        block = glu_block(1 - s, piece)
        wide["glu", "y", piece] = start(copy(("glu", "y", piece), block, block, "y"))

    def pw_rows_at(piece):
        return pl.ds(pl.multiple_of((g * 2 + piece) * pw_part, 16), pw_part)

    def pw_send(piece):
        src = pw_ref.at[pw_rows_at(piece), :]
        dst = pw_all.at[s, pw_rows_at(piece), :]
        wide["pw", "x", piece] = start(copy(("pw", "x", piece), src, dst, "x"))

    def pw_forward(piece):
        wide["pw", "x", piece].wait_recv()
        block = pw_all.at[1 - s, pw_rows_at(piece), :]
        wide["pw", "y", piece] = start(copy(("pw", "y", piece), block, block, "y"))

    def layer(read, at_rows):
        lo, hi = read(0), read(1)
        mean = (jnp.sum(lo, axis=1, keepdims=True) + jnp.sum(hi, axis=1, keepdims=True)) / width
        lo, hi = lo - mean, hi - mean
        var = (jnp.sum(lo * lo, axis=1, keepdims=True) + jnp.sum(hi * hi, axis=1, keepdims=True)) / width
        scale = lax.rsqrt(var + EPS)
        normed[at_rows, :half] = (lo * scale).astype(jnp.bfloat16)
        normed[at_rows, half:] = (hi * scale).astype(jnp.bfloat16)

    z_first("qkv")
    x_send("qkv", "own", f)
    frames_first()
    glu_send(0)
    here = [
        pltpu.make_async_copy(frames_ref, frames_at(f), local_sem.at[0]),
        pltpu.make_async_copy(shard_ref, packed.at[rows_at(f * 2 + s), :], local_sem.at[1]),
        pltpu.make_async_copy(glu_ref, glu_all.at[s], local_sem.at[2]),
        pltpu.make_async_copy(pw_ref, pw_all.at[s], local_sem.at[3]),
    ]
    for c in here:
        c.start()

    def layer_block(name, place):
        swaps[name].wait_recv()
        where = frame_rows(place)
        layer(lambda i: full[i, where, :].astype(jnp.float32), where)

    here[0].wait()
    layer_block("own", f)
    y_forward("qkv", "own", f)
    z_second("qkv")
    frames_second()
    z_first("out")
    y_forward("qkv", "left", left)
    y_forward("qkv", "right", right)
    glu_forward(0)
    z_last("qkv")
    x_send("out", "own", f)
    glu_send(1)
    pw_send(0)
    pw_send(1)
    layer_block("left", left)
    layer_block("right", right)
    y_forward("qkv", "across", across)
    frames_last()
    y_forward("out", "own", f)
    layer_block("across", across)
    here[1].wait()
    for name in places:
        y_copies["qkv", name].wait_recv()

    @pl.loop(0, ring)
    def _(place):
        where = frame_rows(place)
        for i in range(2):
            kv_all[i, where, :] = jnp.dot(
                normed[where, :], packed[:, (i + 1) * att : (i + 2) * att],
                preferred_element_type=jnp.float32,
            ).astype(jnp.bfloat16)

    z_second("out")
    qkv[...] = jnp.dot(
        normed[frame_rows(f), :], packed[:, :att], preferred_element_type=jnp.float32
    ).astype(jnp.bfloat16)
    glu_forward(1)

    y_forward("out", "left", left)
    y_forward("out", "right", right)
    pw_forward(0)
    z_last("out")

    length = length_ref[0]
    total = kv_all.shape[1]
    valid = lax.broadcasted_iota(jnp.int32, (1, total), 1) < length
    column = lax.broadcasted_iota(jnp.int32, (1, att), 1)
    scale_factor = 1.0 / math.sqrt(HEAD_DIM)
    gathered = jnp.zeros((rows, att), jnp.float32)
    for head in range(att // HEAD_DIM):
        mine = (column >= head * HEAD_DIM) & (column < (head + 1) * HEAD_DIM)
        query = jnp.where(mine, qkv[...].astype(jnp.float32), 0.0).astype(jnp.bfloat16)
        scores = lax.dot_general(
            query, kv_all[0], (((1,), (1,)), ((), ())), preferred_element_type=jnp.float32
        ) * scale_factor
        masked = jnp.where(valid, scores, NEG_FILL)
        top = jnp.max(masked, axis=1, keepdims=True)
        expo = jnp.where(valid, jnp.exp(masked - top), 0.0)
        denom = jnp.sum(expo, axis=1, keepdims=True)
        mixed = jnp.dot(
            expo.astype(jnp.bfloat16), kv_all[1], preferred_element_type=jnp.float32
        )
        gathered = jnp.where(mine, mixed / denom, gathered)
    context[...] = gathered.astype(jnp.bfloat16)

    y_forward("out", "across", across)
    pw_forward(1)
    for name in places:
        y_copies["out", name].wait_recv()
    for i in range(2):
        part[i] = lax.dot_general(
            context[...], packed[i * half : (i + 1) * half, 3 * att :],
            (((1,), (1,)), ((), ())), preferred_element_type=jnp.float32,
        ).astype(jnp.bfloat16)
    summed = start(copy("part", part, part_in, "core"))
    summed.wait_recv()
    for i in range(2):
        both = (part[i].astype(jnp.float32) + part_in[i].astype(jnp.float32)).astype(jnp.bfloat16)
        stream[i] = (full[i, frame_rows(f), :].astype(jnp.float32) + both.astype(jnp.float32)).astype(jnp.bfloat16)
    layer(lambda i: stream[i].astype(jnp.float32), pl.ds(0, rows))

    here[2].wait()
    wide["glu", "y", 0].wait_recv()
    wide["glu", "y", 1].wait_recv()
    live = f * rows + lax.broadcasted_iota(jnp.int32, (rows, 1), 0) < length
    tile_cols = 256

    @pl.loop(0, half // tile_cols)
    def _(tile):
        first = pl.multiple_of(tile * tile_cols, tile_cols)
        pre = []
        for base in (0, half):
            cols = pl.ds(base + first, tile_cols)
            pre.append(
                jnp.dot(normed[:rows, :half], glu_all[0, :, cols], preferred_element_type=jnp.float32)
                + jnp.dot(normed[:rows, half:], glu_all[1, :, cols], preferred_element_type=jnp.float32)
            )
        gated = jnp.where(live, pre[0] * jax.nn.sigmoid(pre[1]), 0.0).astype(jnp.bfloat16)
        cols = pl.ds(first, tile_cols)
        edge[0, :, cols] = gated[:HALO]
        edge[1, :, cols] = gated[rows - HALO :]
        padded[pl.ds(HALO, rows), cols] = gated.astype(jnp.float32)

    tail = start(copy("tail", edge.at[1], edge_in.at[0], "right"))
    head = start(copy("head", edge.at[0], edge_in.at[1], "left"))
    tail.wait_recv()
    head.wait_recv()
    has_left = jnp.where(f > 0, 1.0, 0.0)
    has_right = jnp.where(f < ring - 1, 1.0, 0.0)
    padded[:HALO, :] = edge_in[0].astype(jnp.float32) * has_left
    padded[HALO + rows :, :] = edge_in[1].astype(jnp.float32) * has_right

    lanes = 128
    step_rows = 64

    @pl.loop(0, half // lanes)
    def _(tile):
        cols = pl.ds(pl.multiple_of(tile * lanes, lanes), lanes)
        taps = taps_ref[:, cols].astype(jnp.float32)
        for first in range(0, rows, step_rows):
            depth = jnp.zeros((step_rows, lanes), jnp.float32)
            for tap in range(KERNEL):
                at_row = first + tap + HALO - KERNEL // 2
                depth = depth + padded[at_row : at_row + step_rows, cols] * taps[tap : tap + 1]
            hidden[first : first + step_rows, cols] = (depth * jax.nn.sigmoid(depth)).astype(jnp.bfloat16)

    here[3].wait()
    wide["pw", "y", 0].wait_recv()
    wide["pw", "y", 1].wait_recv()
    conv[1] = jnp.dot(
        hidden[...], pw_all[1 - h], preferred_element_type=jnp.float32
    ).astype(jnp.bfloat16)
    given = start(copy("conv", conv.at[1], conv_in, "core"))
    conv[0] = jnp.dot(
        hidden[...], pw_all[h], preferred_element_type=jnp.float32
    ).astype(jnp.bfloat16)
    given.wait_recv()
    both = (conv[0].astype(jnp.float32) + conv_in[...].astype(jnp.float32)).astype(jnp.bfloat16)
    out_ref[...] = (stream[h].astype(jnp.float32) + both.astype(jnp.float32)).astype(jnp.bfloat16)
    for c in started:
        c.wait_send()


def fused(frames_in, lengths, w_query, w_key, w_value, w_out, w_glu, dw_kernel, w_pw):
    rows, half = frames_in.shape[1:]
    att = w_query.shape[1]
    width = 2 * half
    ring = lax.axis_size("frames")
    shard = jnp.concatenate([w_query, w_key, w_value, w_out.T], axis=1)
    glu = w_glu.reshape(w_glu.shape[0], 2 * w_glu.shape[2])
    bf16, f32 = jnp.bfloat16, jnp.float32
    vmem = pl.BlockSpec(memory_space=pltpu.VMEM)
    anywhere = pl.BlockSpec(memory_space=pl.ANY)
    copies = 48
    result = pl.pallas_call(
        block_kernel,
        out_shape=jax.ShapeDtypeStruct((rows, half), bf16),
        in_specs=[anywhere, pl.BlockSpec(memory_space=pltpu.SMEM), anywhere, anywhere, vmem, anywhere],
        out_specs=vmem,
        scratch_shapes=[
            pltpu.VMEM((2, ring * rows, half), bf16),
            pltpu.VMEM((width, 4 * att), bf16),
            pltpu.VMEM((2,) + glu.shape, bf16),
            pltpu.VMEM((2,) + w_pw.shape, bf16),
            pltpu.VMEM((ring * rows, width), bf16),
            pltpu.VMEM((rows, att), bf16),
            pltpu.VMEM((2, ring * rows, att), bf16),
            pltpu.VMEM((rows, att), bf16),
            pltpu.VMEM((2, rows, half), bf16),
            pltpu.VMEM((2, rows, half), bf16),
            pltpu.VMEM((2, rows, half), bf16),
            pltpu.VMEM((rows + 2 * HALO, half), f32),
            pltpu.VMEM((2, HALO, half), bf16),
            pltpu.VMEM((2, HALO, half), bf16),
            pltpu.VMEM((rows, half), bf16),
            pltpu.VMEM((2, rows, half), bf16),
            pltpu.VMEM((rows, half), bf16),
            pltpu.SemaphoreType.DMA((4,)),
            pltpu.SemaphoreType.DMA((copies,)),
            pltpu.SemaphoreType.DMA((copies,)),
        ],
        compiler_params=pltpu.CompilerParams(
            collective_id=0, has_side_effects=True, vmem_limit_bytes=52 * 2**20
        ),
        cost_estimate=pl.CostEstimate(
            flops=2 * rows * width * (3 * att + 4 * half), bytes_accessed=2 * width * (4 * att + 6 * half),
            transcendentals=rows * rows * ring * 4,
        ),
    )(frames_in[0], lengths, shard, glu, dw_kernel, w_pw)
    return result[None]


def fits(mesh):
    sizes = dict(mesh.shape)
    return sizes["groups"] == 2 and sizes["fsdp"] == 2 and sizes["heads"] == 2 and sizes["frames"] == 4


def solution(mesh):
    in_specs = (
        P(("groups", "fsdp"), "frames", "heads"),
        P(("groups", "fsdp")),
        P(("frames", "fsdp"), "heads"),
        P(("frames", "fsdp"), "heads"),
        P(("frames", "fsdp"), "heads"),
        P("heads", ("frames", "fsdp")),
        P("fsdp", None, "heads"),
        P(None, "heads"),
        P("heads", "fsdp"),
    )
    out_specs = P(("groups", "fsdp"), "frames", "heads")
    body = fused if fits(mesh) else shards
    return jax.shard_map(body, mesh=mesh, in_specs=in_specs, out_specs=out_specs, check_vma=False)
```

```python
import functools
import math

import jax
import jax.numpy as jnp
from jax import lax
from jax.experimental import pallas as pl
from jax.experimental.pallas import tpu as pltpu
from jax.sharding import PartitionSpec as P

HEAD_DIM = 96
KERNEL = 31


EPS = 1e-05
NEG_FILL = -1e30


def padded_2(cells, sides, width):
    for axis, dim in sides:
        count = lax.axis_size(axis)
        ends = count - 1
        head = lax.slice_in_dim(cells, 0, width, axis=dim)
        tail = lax.slice_in_dim(cells, cells.shape[dim] - width, cells.shape[dim], axis=dim)
        cells = jnp.concatenate(
            [
                lax.ppermute(tail, axis, [(i, (i + 1) % count) for i in range(ends)]),
                cells,
                lax.ppermute(head, axis, [((i + 1) % count, i) for i in range(ends)]),
            ],
            axis=dim,
        )
    return cells


def layer_norm(rows):
    values = rows.astype(jnp.float32)
    mean_row = jnp.mean(values, axis=-1, keepdims=True)
    centred = values - mean_row
    variance = jnp.mean(centred * centred, axis=-1, keepdims=True)
    return centred * lax.rsqrt(variance + EPS)


def shards(frames_in, lengths, w_query, w_key, w_value, w_out, w_glu, dw_kernel, w_pw):
    full_rows = lax.all_gather(frames_in, "heads", axis=2, tiled=True)[0]
    frame_count = full_rows.shape[0]
    half_width = frames_in.shape[2]
    own_start = lax.axis_index("heads") * half_width
    normed = layer_norm(full_rows).astype(jnp.bfloat16)
    att_cols = w_query.shape[1]
    pieces = (
        lax.all_gather(w_query, ("frames", "fsdp"), axis=0, tiled=True),
        lax.all_gather(w_key, ("frames", "fsdp"), axis=0, tiled=True),
        lax.all_gather(w_value, ("frames", "fsdp"), axis=0, tiled=True),
    )
    sliced = normed
    projected = tuple(
        (jnp.dot(sliced, piece_part, preferred_element_type=jnp.float32) for piece_part in pieces)
    )
    head_count = att_cols // HEAD_DIM
    queries = projected[0].astype(jnp.bfloat16).reshape(frame_count, head_count, HEAD_DIM)
    key_rows = projected[1].astype(jnp.bfloat16)
    value_rows = projected[2].astype(jnp.bfloat16)
    length = lengths[0]
    scale_factor = 1.0 / math.sqrt(HEAD_DIM)
    start_max = jnp.full((frame_count, head_count), NEG_FILL, jnp.float32)
    pieces = (
        lax.all_gather(key_rows, "frames", axis=0, tiled=True),
        lax.all_gather(value_rows, "frames", axis=0, tiled=True),
    )
    key_block = pieces[0].reshape(-1, head_count, HEAD_DIM)
    value_block = pieces[1].reshape(-1, head_count, HEAD_DIM)
    block_rows = key_block.shape[0]
    scores = (
        jnp.einsum("qhd,khd->qhk", queries, key_block, preferred_element_type=jnp.float32)
        * scale_factor
    )
    valid = jnp.arange(block_rows, dtype=jnp.int32) < length
    masked = jnp.where(valid, scores, NEG_FILL)
    new_max = jnp.maximum(start_max, jnp.max(masked, axis=2))
    expo = jnp.where(valid, jnp.exp(masked - new_max[:, :, None]), 0.0)
    new_sum = jnp.sum(expo, axis=2)
    block_acc = jnp.einsum(
        "qhk,khd->qhd", expo.astype(jnp.bfloat16), value_block, preferred_element_type=jnp.float32
    )
    context = (block_acc / new_sum[:, :, None]).reshape(frame_count, att_cols).astype(jnp.bfloat16)
    partial_value = jnp.dot(
        context,
        lax.all_gather(w_out, ("frames", "fsdp"), axis=1, tiled=True),
        preferred_element_type=jnp.float32,
    )
    total = lax.psum(partial_value.astype(jnp.bfloat16), "heads").astype(jnp.float32)
    stream_full = (full_rows.astype(jnp.float32) + total).astype(jnp.bfloat16)
    stream_own = lax.dynamic_slice_in_dim(stream_full, own_start, half_width, 1)
    normed_two = layer_norm(stream_full).astype(jnp.bfloat16)
    channels = w_glu.shape[2]
    sliced = normed_two
    glu_pre = jnp.einsum(
        "td,dgc->tgc",
        sliced,
        lax.all_gather(w_glu, "fsdp", axis=0, tiled=True),
        preferred_element_type=jnp.float32,
    )
    positions = lax.axis_index("frames") * frame_count + jnp.arange(frame_count, dtype=jnp.int32)
    live = positions < length
    gated = jnp.where(
        live[:, None], glu_pre[:, 0, :] * jax.nn.sigmoid(glu_pre[:, 1, :]), 0.0
    ).astype(jnp.bfloat16)
    padded = padded_2(gated, (("frames", 0),), KERNEL // 2)
    depth = jnp.zeros((frame_count, channels), jnp.float32)
    for tap_index in range(KERNEL):
        depth = depth + padded[tap_index : tap_index + frame_count].astype(jnp.float32) * dw_kernel[
            tap_index
        ].astype(jnp.float32)
    hidden = (depth * jax.nn.sigmoid(depth)).astype(jnp.bfloat16)
    conv_part = jnp.dot(
        hidden, lax.all_gather(w_pw, "fsdp", axis=1, tiled=True), preferred_element_type=jnp.float32
    )
    conv_half = lax.psum_scatter(
        conv_part.astype(jnp.bfloat16), "heads", scatter_dimension=1, tiled=True
    ).astype(jnp.float32)
    result = (stream_own.astype(jnp.float32) + conv_half).astype(jnp.bfloat16)
    return result[None]


MESH = pl.DeviceIdType.MESH
HALO = 16


def block_kernel(
    frames_ref, length_ref, shard_ref, glu_ref, taps_ref, pw_ref, out_ref,
    full, packed, glu_all, pw_all, normed, qkv, kv_all, context,
    part, part_in, stream, padded, edge, edge_in, hidden, conv, conv_in,
    local_sem, send_sem, recv_sem,
):
    rows, half = frames_ref.shape
    width = 2 * half
    shard_rows = shard_ref.shape[0]
    att = shard_ref.shape[1] // 4
    g, f = lax.axis_index("groups"), lax.axis_index("frames")
    s, h = lax.axis_index("fsdp"), lax.axis_index("heads")
    ring = lax.axis_size("frames")
    right, left = lax.rem(f + 1, ring), lax.rem(f + ring - 1, ring)
    across = lax.rem(f + 2, ring)
    peers = {
        "right": {"frames": right}, "left": {"frames": left},
        "x": {"fsdp": 1 - s}, "y": {"groups": 1 - g}, "core": {"heads": 1 - h},
    }
    names = {}

    def copy(name, src, dst, to):
        slot = names.setdefault(name, len(names))
        return pltpu.make_async_remote_copy(
            src_ref=src, dst_ref=dst, send_sem=send_sem.at[slot], recv_sem=recv_sem.at[slot],
            device_id=peers[to], device_id_type=MESH,
        )

    barrier = pltpu.get_barrier_semaphore()
    for to in peers:
        pl.semaphore_signal(barrier, inc=1, device_id=peers[to], device_id_type=MESH)
    pl.semaphore_wait(barrier, len(peers))

    started = []

    def start(c):
        c.start()
        started.append(c)
        return c

    def rows_at(index, first=0, count=shard_rows):
        return pl.ds(pl.multiple_of(index * shard_rows + first, 16), count)

    mid = shard_rows // 2
    own_half = g * mid
    columns = {"qkv": pl.ds(0, 3 * att), "out": pl.ds(3 * att, att)}

    def at(kind, place, axis_s, first=0, count=shard_rows):
        return packed.at[rows_at(place * 2 + axis_s, first, count), columns[kind]]

    def own_src(kind, first=0, count=shard_rows):
        return shard_ref.at[pl.ds(pl.multiple_of(first, 16), count), columns[kind]]

    def frame_rows(place, first=0, count=rows):
        return pl.ds(pl.multiple_of(place * rows + first, 16), count)

    def frames_at(place, first=0, count=rows):
        return full.at[h, frame_rows(place, first, count), :]

    swaps = {"own": start(copy(("frames", "own"), frames_ref, frames_at(f), "core"))}
    frame_copies = {}

    def frames_first():
        for to in ("right", "left"):
            frame_copies[to, 0] = start(copy(("frames", to, 0), frames_ref, frames_at(f), to))

    def frames_swap(name, place):
        block = frames_at(place)
        swaps[name] = start(copy(("frames", name), block, block, "core"))

    def frames_second():
        frame_mid = rows // 2
        frame_copies["right", 0].wait_recv()
        block = frames_at(left, 0, frame_mid)
        frame_copies["right", 1] = start(copy(("frames", "right", 1), block, block, "right"))
        frames_swap("left", left)
        frame_copies["left", 0].wait_recv()
        block = frames_at(right, frame_mid, frame_mid)
        frame_copies["left", 1] = start(copy(("frames", "left", 1), block, block, "left"))
        frames_swap("right", right)

    def frames_last():
        frame_copies["right", 1].wait_recv()
        frame_copies["left", 1].wait_recv()
        frames_swap("across", across)

    z_copies, x_copies, y_copies = {}, {}, {}

    def z_first(kind):
        for to in ("right", "left"):
            z_copies[kind, to, 0] = start(
                copy((kind, to, 0), own_src(kind), at(kind, f, s), to)
            )

    def x_send(kind, place_name, place):
        src = own_src(kind, own_half, mid) if place_name == "own" else at(kind, place, s, own_half, mid)
        x_copies[kind, place_name] = start(
            copy((kind, "x", place_name), src, at(kind, place, s, own_half, mid), "x")
        )

    def y_forward(kind, place_name, place):
        x_copies[kind, place_name].wait_recv()
        block = at(kind, place, 1 - s, own_half, mid)
        y_copies[kind, place_name] = start(copy((kind, "y", place_name), block, block, "y"))

    def z_second(kind):
        z_copies[kind, "right", 0].wait_recv()
        top = at(kind, left, s, 0, mid)
        z_copies[kind, "right", 1] = start(copy((kind, "right", 1), top, top, "right"))
        x_send(kind, "left", left)
        z_copies[kind, "left", 0].wait_recv()
        low = at(kind, right, s, mid, mid)
        z_copies[kind, "left", 1] = start(copy((kind, "left", 1), low, low, "left"))
        x_send(kind, "right", right)

    def z_last(kind):
        z_copies[kind, "right", 1].wait_recv()
        z_copies[kind, "left", 1].wait_recv()
        x_send(kind, "across", across)

    places = {"own": f, "left": left, "right": right, "across": across}

    glu_rows = glu_ref.shape[0]
    glu_part = glu_rows // 4
    pw_rows = pw_ref.shape[0]
    pw_part = pw_rows // 4
    wide = {}

    def glu_block(axis_s, piece):
        return glu_all.at[axis_s, pl.ds(pl.multiple_of((g * 2 + piece) * glu_part, 16), glu_part), :]

    def glu_send(piece):
        src = glu_ref.at[pl.ds(pl.multiple_of((g * 2 + piece) * glu_part, 16), glu_part), :]
        wide["glu", "x", piece] = start(copy(("glu", "x", piece), src, glu_block(s, piece), "x"))

    def glu_forward(piece):
        wide["glu", "x", piece].wait_recv()
        block = glu_block(1 - s, piece)
        wide["glu", "y", piece] = start(copy(("glu", "y", piece), block, block, "y"))

    def pw_rows_at(piece):
        return pl.ds(pl.multiple_of((g * 2 + piece) * pw_part, 16), pw_part)

    def pw_send(piece):
        src = pw_ref.at[pw_rows_at(piece), :]
        dst = pw_all.at[s, pw_rows_at(piece), :]
        wide["pw", "x", piece] = start(copy(("pw", "x", piece), src, dst, "x"))

    def pw_forward(piece):
        wide["pw", "x", piece].wait_recv()
        block = pw_all.at[1 - s, pw_rows_at(piece), :]
        wide["pw", "y", piece] = start(copy(("pw", "y", piece), block, block, "y"))

    def layer(read, at_rows):
        lo, hi = read(0), read(1)
        mean = (jnp.sum(lo, axis=1, keepdims=True) + jnp.sum(hi, axis=1, keepdims=True)) / width
        lo, hi = lo - mean, hi - mean
        var = (jnp.sum(lo * lo, axis=1, keepdims=True) + jnp.sum(hi * hi, axis=1, keepdims=True)) / width
        scale = lax.rsqrt(var + EPS)
        normed[at_rows, :half] = (lo * scale).astype(jnp.bfloat16)
        normed[at_rows, half:] = (hi * scale).astype(jnp.bfloat16)

    z_first("qkv")
    x_send("qkv", "own", f)
    frames_first()
    glu_send(0)
    here = [
        pltpu.make_async_copy(frames_ref, frames_at(f), local_sem.at[0]),
        pltpu.make_async_copy(shard_ref, packed.at[rows_at(f * 2 + s), :], local_sem.at[1]),
        pltpu.make_async_copy(glu_ref, glu_all.at[s], local_sem.at[2]),
        pltpu.make_async_copy(pw_ref, pw_all.at[s], local_sem.at[3]),
    ]
    for c in here:
        c.start()

    def layer_block(name, place):
        swaps[name].wait_recv()
        where = frame_rows(place)
        layer(lambda i: full[i, where, :].astype(jnp.float32), where)

    here[0].wait()
    layer_block("own", f)
    y_forward("qkv", "own", f)
    z_second("qkv")
    frames_second()
    z_first("out")
    y_forward("qkv", "left", left)
    y_forward("qkv", "right", right)
    glu_forward(0)
    z_last("qkv")
    x_send("out", "own", f)
    glu_send(1)
    layer_block("left", left)
    layer_block("right", right)
    y_forward("qkv", "across", across)
    frames_last()
    y_forward("out", "own", f)
    layer_block("across", across)
    here[1].wait()
    for name in places:
        y_copies["qkv", name].wait_recv()

    @pl.loop(0, ring)
    def _(place):
        where = frame_rows(place)
        for i in range(2):
            kv_all[i, where, :] = jnp.dot(
                normed[where, :], packed[:, (i + 1) * att : (i + 2) * att],
                preferred_element_type=jnp.float32,
            ).astype(jnp.bfloat16)

    z_second("out")
    pw_send(0)
    qkv[...] = jnp.dot(
        normed[frame_rows(f), :], packed[:, :att], preferred_element_type=jnp.float32
    ).astype(jnp.bfloat16)
    glu_forward(1)

    y_forward("out", "left", left)
    y_forward("out", "right", right)
    z_last("out")
    pw_send(1)

    length = length_ref[0]
    total = kv_all.shape[1]
    valid = lax.broadcasted_iota(jnp.int32, (1, total), 1) < length
    column = lax.broadcasted_iota(jnp.int32, (1, att), 1)
    scale_factor = 1.0 / math.sqrt(HEAD_DIM)
    gathered = jnp.zeros((rows, att), jnp.float32)
    for head in range(att // HEAD_DIM):
        mine = (column >= head * HEAD_DIM) & (column < (head + 1) * HEAD_DIM)
        query = jnp.where(mine, qkv[...].astype(jnp.float32), 0.0).astype(jnp.bfloat16)
        scores = lax.dot_general(
            query, kv_all[0], (((1,), (1,)), ((), ())), preferred_element_type=jnp.float32
        ) * scale_factor
        masked = jnp.where(valid, scores, NEG_FILL)
        top = jnp.max(masked, axis=1, keepdims=True)
        expo = jnp.where(valid, jnp.exp(masked - top), 0.0)
        denom = jnp.sum(expo, axis=1, keepdims=True)
        mixed = jnp.dot(
            expo.astype(jnp.bfloat16), kv_all[1], preferred_element_type=jnp.float32
        )
        gathered = jnp.where(mine, mixed / denom, gathered)
    context[...] = gathered.astype(jnp.bfloat16)

    y_forward("out", "across", across)
    pw_forward(0)
    for name in places:
        y_copies["out", name].wait_recv()
    for i in range(2):
        part[i] = lax.dot_general(
            context[...], packed[i * half : (i + 1) * half, 3 * att :],
            (((1,), (1,)), ((), ())), preferred_element_type=jnp.float32,
        ).astype(jnp.bfloat16)
    summed = start(copy("part", part, part_in, "core"))
    pw_forward(1)
    summed.wait_recv()
    for i in range(2):
        both = (part[i].astype(jnp.float32) + part_in[i].astype(jnp.float32)).astype(jnp.bfloat16)
        stream[i] = (full[i, frame_rows(f), :].astype(jnp.float32) + both.astype(jnp.float32)).astype(jnp.bfloat16)
    layer(lambda i: stream[i].astype(jnp.float32), pl.ds(0, rows))

    here[2].wait()
    wide["glu", "y", 0].wait_recv()
    wide["glu", "y", 1].wait_recv()
    live = f * rows + lax.broadcasted_iota(jnp.int32, (rows, 1), 0) < length
    tile_cols = 256

    @pl.loop(0, half // tile_cols)
    def _(tile):
        first = pl.multiple_of(tile * tile_cols, tile_cols)
        pre = []
        for base in (0, half):
            cols = pl.ds(base + first, tile_cols)
            pre.append(
                jnp.dot(normed[:rows, :half], glu_all[0, :, cols], preferred_element_type=jnp.float32)
                + jnp.dot(normed[:rows, half:], glu_all[1, :, cols], preferred_element_type=jnp.float32)
            )
        gated = jnp.where(live, pre[0] * jax.nn.sigmoid(pre[1]), 0.0).astype(jnp.bfloat16)
        cols = pl.ds(first, tile_cols)
        edge[0, :, cols] = gated[:HALO]
        edge[1, :, cols] = gated[rows - HALO :]
        padded[pl.ds(HALO, rows), cols] = gated.astype(jnp.float32)

    tail = start(copy("tail", edge.at[1], edge_in.at[0], "right"))
    head = start(copy("head", edge.at[0], edge_in.at[1], "left"))
    tail.wait_recv()
    head.wait_recv()
    has_left = jnp.where(f > 0, 1.0, 0.0)
    has_right = jnp.where(f < ring - 1, 1.0, 0.0)
    padded[:HALO, :] = edge_in[0].astype(jnp.float32) * has_left
    padded[HALO + rows :, :] = edge_in[1].astype(jnp.float32) * has_right

    lanes = 128
    step_rows = 64

    @pl.loop(0, half // lanes)
    def _(tile):
        cols = pl.ds(pl.multiple_of(tile * lanes, lanes), lanes)
        taps = taps_ref[:, cols].astype(jnp.float32)
        for first in range(0, rows, step_rows):
            depth = jnp.zeros((step_rows, lanes), jnp.float32)
            for tap in range(KERNEL):
                at_row = first + tap + HALO - KERNEL // 2
                depth = depth + padded[at_row : at_row + step_rows, cols] * taps[tap : tap + 1]
            hidden[first : first + step_rows, cols] = (depth * jax.nn.sigmoid(depth)).astype(jnp.bfloat16)

    here[3].wait()
    wide["pw", "y", 0].wait_recv()
    wide["pw", "y", 1].wait_recv()
    conv[1] = jnp.dot(
        hidden[...], pw_all[1 - h], preferred_element_type=jnp.float32
    ).astype(jnp.bfloat16)
    given = start(copy("conv", conv.at[1], conv_in, "core"))
    conv[0] = jnp.dot(
        hidden[...], pw_all[h], preferred_element_type=jnp.float32
    ).astype(jnp.bfloat16)
    given.wait_recv()
    both = (conv[0].astype(jnp.float32) + conv_in[...].astype(jnp.float32)).astype(jnp.bfloat16)
    out_ref[...] = (stream[h].astype(jnp.float32) + both.astype(jnp.float32)).astype(jnp.bfloat16)
    for c in started:
        c.wait_send()


def fused(frames_in, lengths, w_query, w_key, w_value, w_out, w_glu, dw_kernel, w_pw):
    rows, half = frames_in.shape[1:]
    att = w_query.shape[1]
    width = 2 * half
    ring = lax.axis_size("frames")
    shard = jnp.concatenate([w_query, w_key, w_value, w_out.T], axis=1)
    glu = w_glu.reshape(w_glu.shape[0], 2 * w_glu.shape[2])
    bf16, f32 = jnp.bfloat16, jnp.float32
    vmem = pl.BlockSpec(memory_space=pltpu.VMEM)
    anywhere = pl.BlockSpec(memory_space=pl.ANY)
    copies = 48
    result = pl.pallas_call(
        block_kernel,
        out_shape=jax.ShapeDtypeStruct((rows, half), bf16),
        in_specs=[anywhere, pl.BlockSpec(memory_space=pltpu.SMEM), anywhere, anywhere, vmem, anywhere],
        out_specs=vmem,
        scratch_shapes=[
            pltpu.VMEM((2, ring * rows, half), bf16),
            pltpu.VMEM((width, 4 * att), bf16),
            pltpu.VMEM((2,) + glu.shape, bf16),
            pltpu.VMEM((2,) + w_pw.shape, bf16),
            pltpu.VMEM((ring * rows, width), bf16),
            pltpu.VMEM((rows, att), bf16),
            pltpu.VMEM((2, ring * rows, att), bf16),
            pltpu.VMEM((rows, att), bf16),
            pltpu.VMEM((2, rows, half), bf16),
            pltpu.VMEM((2, rows, half), bf16),
            pltpu.VMEM((2, rows, half), bf16),
            pltpu.VMEM((rows + 2 * HALO, half), f32),
            pltpu.VMEM((2, HALO, half), bf16),
            pltpu.VMEM((2, HALO, half), bf16),
            pltpu.VMEM((rows, half), bf16),
            pltpu.VMEM((2, rows, half), bf16),
            pltpu.VMEM((rows, half), bf16),
            pltpu.SemaphoreType.DMA((4,)),
            pltpu.SemaphoreType.DMA((copies,)),
            pltpu.SemaphoreType.DMA((copies,)),
        ],
        compiler_params=pltpu.CompilerParams(
            collective_id=0, has_side_effects=True, vmem_limit_bytes=52 * 2**20
        ),
        cost_estimate=pl.CostEstimate(
            flops=2 * rows * width * (3 * att + 4 * half), bytes_accessed=2 * width * (4 * att + 6 * half),
            transcendentals=rows * rows * ring * 4,
        ),
    )(frames_in[0], lengths, shard, glu, dw_kernel, w_pw)
    return result[None]


def fits(mesh):
    sizes = dict(mesh.shape)
    return sizes["groups"] == 2 and sizes["fsdp"] == 2 and sizes["heads"] == 2 and sizes["frames"] == 4


def solution(mesh):
    in_specs = (
        P(("groups", "fsdp"), "frames", "heads"),
        P(("groups", "fsdp")),
        P(("frames", "fsdp"), "heads"),
        P(("frames", "fsdp"), "heads"),
        P(("frames", "fsdp"), "heads"),
        P("heads", ("frames", "fsdp")),
        P("fsdp", None, "heads"),
        P(None, "heads"),
        P("heads", "fsdp"),
    )
    out_specs = P(("groups", "fsdp"), "frames", "heads")
    body = fused if fits(mesh) else shards
    return jax.shard_map(body, mesh=mesh, in_specs=in_specs, out_specs=out_specs, check_vma=False)
```

```python
import functools
import math

import jax
import jax.numpy as jnp
from jax import lax
from jax.experimental import pallas as pl
from jax.experimental.pallas import tpu as pltpu
from jax.sharding import PartitionSpec as P

HEAD_DIM = 96
KERNEL = 31


EPS = 1e-05
NEG_FILL = -1e30


def padded_2(cells, sides, width):
    for axis, dim in sides:
        count = lax.axis_size(axis)
        ends = count - 1
        head = lax.slice_in_dim(cells, 0, width, axis=dim)
        tail = lax.slice_in_dim(cells, cells.shape[dim] - width, cells.shape[dim], axis=dim)
        cells = jnp.concatenate(
            [
                lax.ppermute(tail, axis, [(i, (i + 1) % count) for i in range(ends)]),
                cells,
                lax.ppermute(head, axis, [((i + 1) % count, i) for i in range(ends)]),
            ],
            axis=dim,
        )
    return cells


def layer_norm(rows):
    values = rows.astype(jnp.float32)
    mean_row = jnp.mean(values, axis=-1, keepdims=True)
    centred = values - mean_row
    variance = jnp.mean(centred * centred, axis=-1, keepdims=True)
    return centred * lax.rsqrt(variance + EPS)


def shards(frames_in, lengths, w_query, w_key, w_value, w_out, w_glu, dw_kernel, w_pw):
    full_rows = lax.all_gather(frames_in, "heads", axis=2, tiled=True)[0]
    frame_count = full_rows.shape[0]
    half_width = frames_in.shape[2]
    own_start = lax.axis_index("heads") * half_width
    normed = layer_norm(full_rows).astype(jnp.bfloat16)
    att_cols = w_query.shape[1]
    pieces = (
        lax.all_gather(w_query, ("frames", "fsdp"), axis=0, tiled=True),
        lax.all_gather(w_key, ("frames", "fsdp"), axis=0, tiled=True),
        lax.all_gather(w_value, ("frames", "fsdp"), axis=0, tiled=True),
    )
    sliced = normed
    projected = tuple(
        (jnp.dot(sliced, piece_part, preferred_element_type=jnp.float32) for piece_part in pieces)
    )
    head_count = att_cols // HEAD_DIM
    queries = projected[0].astype(jnp.bfloat16).reshape(frame_count, head_count, HEAD_DIM)
    key_rows = projected[1].astype(jnp.bfloat16)
    value_rows = projected[2].astype(jnp.bfloat16)
    length = lengths[0]
    scale_factor = 1.0 / math.sqrt(HEAD_DIM)
    start_max = jnp.full((frame_count, head_count), NEG_FILL, jnp.float32)
    pieces = (
        lax.all_gather(key_rows, "frames", axis=0, tiled=True),
        lax.all_gather(value_rows, "frames", axis=0, tiled=True),
    )
    key_block = pieces[0].reshape(-1, head_count, HEAD_DIM)
    value_block = pieces[1].reshape(-1, head_count, HEAD_DIM)
    block_rows = key_block.shape[0]
    scores = (
        jnp.einsum("qhd,khd->qhk", queries, key_block, preferred_element_type=jnp.float32)
        * scale_factor
    )
    valid = jnp.arange(block_rows, dtype=jnp.int32) < length
    masked = jnp.where(valid, scores, NEG_FILL)
    new_max = jnp.maximum(start_max, jnp.max(masked, axis=2))
    expo = jnp.where(valid, jnp.exp(masked - new_max[:, :, None]), 0.0)
    new_sum = jnp.sum(expo, axis=2)
    block_acc = jnp.einsum(
        "qhk,khd->qhd", expo.astype(jnp.bfloat16), value_block, preferred_element_type=jnp.float32
    )
    context = (block_acc / new_sum[:, :, None]).reshape(frame_count, att_cols).astype(jnp.bfloat16)
    partial_value = jnp.dot(
        context,
        lax.all_gather(w_out, ("frames", "fsdp"), axis=1, tiled=True),
        preferred_element_type=jnp.float32,
    )
    total = lax.psum(partial_value.astype(jnp.bfloat16), "heads").astype(jnp.float32)
    stream_full = (full_rows.astype(jnp.float32) + total).astype(jnp.bfloat16)
    stream_own = lax.dynamic_slice_in_dim(stream_full, own_start, half_width, 1)
    normed_two = layer_norm(stream_full).astype(jnp.bfloat16)
    channels = w_glu.shape[2]
    sliced = normed_two
    glu_pre = jnp.einsum(
        "td,dgc->tgc",
        sliced,
        lax.all_gather(w_glu, "fsdp", axis=0, tiled=True),
        preferred_element_type=jnp.float32,
    )
    positions = lax.axis_index("frames") * frame_count + jnp.arange(frame_count, dtype=jnp.int32)
    live = positions < length
    gated = jnp.where(
        live[:, None], glu_pre[:, 0, :] * jax.nn.sigmoid(glu_pre[:, 1, :]), 0.0
    ).astype(jnp.bfloat16)
    padded = padded_2(gated, (("frames", 0),), KERNEL // 2)
    depth = jnp.zeros((frame_count, channels), jnp.float32)
    for tap_index in range(KERNEL):
        depth = depth + padded[tap_index : tap_index + frame_count].astype(jnp.float32) * dw_kernel[
            tap_index
        ].astype(jnp.float32)
    hidden = (depth * jax.nn.sigmoid(depth)).astype(jnp.bfloat16)
    conv_part = jnp.dot(
        hidden, lax.all_gather(w_pw, "fsdp", axis=1, tiled=True), preferred_element_type=jnp.float32
    )
    conv_half = lax.psum_scatter(
        conv_part.astype(jnp.bfloat16), "heads", scatter_dimension=1, tiled=True
    ).astype(jnp.float32)
    result = (stream_own.astype(jnp.float32) + conv_half).astype(jnp.bfloat16)
    return result[None]


MESH = pl.DeviceIdType.MESH
HALO = 16


def block_kernel(
    frames_ref, length_ref, shard_ref, glu_ref, taps_ref, pw_ref, out_ref,
    full, packed, glu_all, pw_all, normed, qkv, kv_all, context,
    part, part_in, stream, padded, edge, edge_in, hidden, conv, conv_in,
    local_sem, send_sem, recv_sem,
):
    rows, half = frames_ref.shape
    width = 2 * half
    shard_rows = shard_ref.shape[0]
    att = shard_ref.shape[1] // 4
    g, f = lax.axis_index("groups"), lax.axis_index("frames")
    s, h = lax.axis_index("fsdp"), lax.axis_index("heads")
    ring = lax.axis_size("frames")
    right, left = lax.rem(f + 1, ring), lax.rem(f + ring - 1, ring)
    across = lax.rem(f + 2, ring)
    peers = {
        "right": {"frames": right}, "left": {"frames": left},
        "x": {"fsdp": 1 - s}, "y": {"groups": 1 - g}, "core": {"heads": 1 - h},
    }
    names = {}

    def copy(name, src, dst, to):
        slot = names.setdefault(name, len(names))
        return pltpu.make_async_remote_copy(
            src_ref=src, dst_ref=dst, send_sem=send_sem.at[slot], recv_sem=recv_sem.at[slot],
            device_id=peers[to], device_id_type=MESH,
        )

    barrier = pltpu.get_barrier_semaphore()
    for to in peers:
        pl.semaphore_signal(barrier, inc=1, device_id=peers[to], device_id_type=MESH)
    pl.semaphore_wait(barrier, len(peers))

    started = []

    def start(c):
        c.start()
        started.append(c)
        return c

    def rows_at(index, first=0, count=shard_rows):
        return pl.ds(pl.multiple_of(index * shard_rows + first, 16), count)

    mid = shard_rows // 2
    own_half = g * mid
    columns = {"qkv": pl.ds(0, 3 * att), "out": pl.ds(3 * att, att)}

    def at(kind, place, axis_s, first=0, count=shard_rows):
        return packed.at[rows_at(place * 2 + axis_s, first, count), columns[kind]]

    def own_src(kind, first=0, count=shard_rows):
        return shard_ref.at[pl.ds(pl.multiple_of(first, 16), count), columns[kind]]

    def frame_rows(place, first=0, count=rows):
        return pl.ds(pl.multiple_of(place * rows + first, 16), count)

    def frames_at(place, first=0, count=rows):
        return full.at[h, frame_rows(place, first, count), :]

    swaps = {"own": start(copy(("frames", "own"), frames_ref, frames_at(f), "core"))}
    frame_copies = {}

    def frames_first():
        for to in ("right", "left"):
            frame_copies[to, 0] = start(copy(("frames", to, 0), frames_ref, frames_at(f), to))

    def frames_swap(name, place):
        block = frames_at(place)
        swaps[name] = start(copy(("frames", name), block, block, "core"))

    def frames_second():
        frame_mid = rows // 2
        frame_copies["right", 0].wait_recv()
        block = frames_at(left, 0, frame_mid)
        frame_copies["right", 1] = start(copy(("frames", "right", 1), block, block, "right"))
        frames_swap("left", left)
        frame_copies["left", 0].wait_recv()
        block = frames_at(right, frame_mid, frame_mid)
        frame_copies["left", 1] = start(copy(("frames", "left", 1), block, block, "left"))
        frames_swap("right", right)

    def frames_last():
        frame_copies["right", 1].wait_recv()
        frame_copies["left", 1].wait_recv()
        frames_swap("across", across)

    z_copies, x_copies, y_copies = {}, {}, {}

    def z_first(kind):
        for to in ("right", "left"):
            z_copies[kind, to, 0] = start(
                copy((kind, to, 0), own_src(kind), at(kind, f, s), to)
            )

    def x_send(kind, place_name, place):
        src = own_src(kind, own_half, mid) if place_name == "own" else at(kind, place, s, own_half, mid)
        x_copies[kind, place_name] = start(
            copy((kind, "x", place_name), src, at(kind, place, s, own_half, mid), "x")
        )

    def y_forward(kind, place_name, place):
        x_copies[kind, place_name].wait_recv()
        block = at(kind, place, 1 - s, own_half, mid)
        y_copies[kind, place_name] = start(copy((kind, "y", place_name), block, block, "y"))

    def z_second(kind):
        z_copies[kind, "right", 0].wait_recv()
        top = at(kind, left, s, 0, mid)
        z_copies[kind, "right", 1] = start(copy((kind, "right", 1), top, top, "right"))
        x_send(kind, "left", left)
        z_copies[kind, "left", 0].wait_recv()
        low = at(kind, right, s, mid, mid)
        z_copies[kind, "left", 1] = start(copy((kind, "left", 1), low, low, "left"))
        x_send(kind, "right", right)

    def z_last(kind):
        z_copies[kind, "right", 1].wait_recv()
        z_copies[kind, "left", 1].wait_recv()
        x_send(kind, "across", across)

    places = {"own": f, "left": left, "right": right, "across": across}

    glu_rows = glu_ref.shape[0]
    glu_part = glu_rows // 4
    pw_rows = pw_ref.shape[0]
    pw_part = pw_rows // 4
    wide = {}

    def glu_block(axis_s, piece):
        return glu_all.at[axis_s, pl.ds(pl.multiple_of((g * 2 + piece) * glu_part, 16), glu_part), :]

    def glu_send(piece):
        src = glu_ref.at[pl.ds(pl.multiple_of((g * 2 + piece) * glu_part, 16), glu_part), :]
        wide["glu", "x", piece] = start(copy(("glu", "x", piece), src, glu_block(s, piece), "x"))

    def glu_forward(piece):
        wide["glu", "x", piece].wait_recv()
        block = glu_block(1 - s, piece)
        wide["glu", "y", piece] = start(copy(("glu", "y", piece), block, block, "y"))

    def pw_rows_at(piece):
        return pl.ds(pl.multiple_of((g * 2 + piece) * pw_part, 16), pw_part)

    def pw_send(piece):
        src = pw_ref.at[pw_rows_at(piece), :]
        dst = pw_all.at[s, pw_rows_at(piece), :]
        wide["pw", "x", piece] = start(copy(("pw", "x", piece), src, dst, "x"))

    def pw_forward(piece):
        wide["pw", "x", piece].wait_recv()
        block = pw_all.at[1 - s, pw_rows_at(piece), :]
        wide["pw", "y", piece] = start(copy(("pw", "y", piece), block, block, "y"))

    def layer(read, at_rows):
        lo, hi = read(0), read(1)
        mean = (jnp.sum(lo, axis=1, keepdims=True) + jnp.sum(hi, axis=1, keepdims=True)) / width
        lo, hi = lo - mean, hi - mean
        var = (jnp.sum(lo * lo, axis=1, keepdims=True) + jnp.sum(hi * hi, axis=1, keepdims=True)) / width
        scale = lax.rsqrt(var + EPS)
        normed[at_rows, :half] = (lo * scale).astype(jnp.bfloat16)
        normed[at_rows, half:] = (hi * scale).astype(jnp.bfloat16)

    z_first("qkv")
    x_send("qkv", "own", f)
    glu_send(0)
    here = [
        pltpu.make_async_copy(frames_ref, frames_at(f), local_sem.at[0]),
        pltpu.make_async_copy(shard_ref, packed.at[rows_at(f * 2 + s), :], local_sem.at[1]),
        pltpu.make_async_copy(glu_ref, glu_all.at[s], local_sem.at[2]),
        pltpu.make_async_copy(pw_ref, pw_all.at[s], local_sem.at[3]),
    ]
    for c in here:
        c.start()

    def layer_block(name, place):
        swaps[name].wait_recv()
        where = frame_rows(place)
        layer(lambda i: full[i, where, :].astype(jnp.float32), where)

    here[0].wait()
    layer_block("own", f)
    y_forward("qkv", "own", f)
    z_second("qkv")
    frames_first()
    y_forward("qkv", "left", left)
    y_forward("qkv", "right", right)
    z_last("qkv")
    glu_forward(0)
    frames_second()
    z_first("out")
    x_send("out", "own", f)
    glu_send(1)
    layer_block("left", left)
    layer_block("right", right)
    y_forward("qkv", "across", across)
    frames_last()
    y_forward("out", "own", f)
    layer_block("across", across)
    here[1].wait()
    for name in places:
        y_copies["qkv", name].wait_recv()

    @pl.loop(0, ring)
    def _(place):
        where = frame_rows(place)
        for i in range(2):
            kv_all[i, where, :] = jnp.dot(
                normed[where, :], packed[:, (i + 1) * att : (i + 2) * att],
                preferred_element_type=jnp.float32,
            ).astype(jnp.bfloat16)

    z_second("out")
    pw_send(0)
    qkv[...] = jnp.dot(
        normed[frame_rows(f), :], packed[:, :att], preferred_element_type=jnp.float32
    ).astype(jnp.bfloat16)
    glu_forward(1)

    y_forward("out", "left", left)
    y_forward("out", "right", right)
    z_last("out")
    pw_send(1)

    length = length_ref[0]
    total = kv_all.shape[1]
    valid = lax.broadcasted_iota(jnp.int32, (1, total), 1) < length
    column = lax.broadcasted_iota(jnp.int32, (1, att), 1)
    scale_factor = 1.0 / math.sqrt(HEAD_DIM)
    gathered = jnp.zeros((rows, att), jnp.float32)
    for head in range(att // HEAD_DIM):
        mine = (column >= head * HEAD_DIM) & (column < (head + 1) * HEAD_DIM)
        query = jnp.where(mine, qkv[...].astype(jnp.float32), 0.0).astype(jnp.bfloat16)
        scores = lax.dot_general(
            query, kv_all[0], (((1,), (1,)), ((), ())), preferred_element_type=jnp.float32
        ) * scale_factor
        masked = jnp.where(valid, scores, NEG_FILL)
        top = jnp.max(masked, axis=1, keepdims=True)
        expo = jnp.where(valid, jnp.exp(masked - top), 0.0)
        denom = jnp.sum(expo, axis=1, keepdims=True)
        mixed = jnp.dot(
            expo.astype(jnp.bfloat16), kv_all[1], preferred_element_type=jnp.float32
        )
        gathered = jnp.where(mine, mixed / denom, gathered)
    context[...] = gathered.astype(jnp.bfloat16)

    y_forward("out", "across", across)
    pw_forward(0)
    for name in places:
        y_copies["out", name].wait_recv()
    for i in range(2):
        part[i] = lax.dot_general(
            context[...], packed[i * half : (i + 1) * half, 3 * att :],
            (((1,), (1,)), ((), ())), preferred_element_type=jnp.float32,
        ).astype(jnp.bfloat16)
    summed = start(copy("part", part, part_in, "core"))
    pw_forward(1)
    summed.wait_recv()
    for i in range(2):
        both = (part[i].astype(jnp.float32) + part_in[i].astype(jnp.float32)).astype(jnp.bfloat16)
        stream[i] = (full[i, frame_rows(f), :].astype(jnp.float32) + both.astype(jnp.float32)).astype(jnp.bfloat16)
    layer(lambda i: stream[i].astype(jnp.float32), pl.ds(0, rows))

    here[2].wait()
    wide["glu", "y", 0].wait_recv()
    wide["glu", "y", 1].wait_recv()
    live = f * rows + lax.broadcasted_iota(jnp.int32, (rows, 1), 0) < length
    tile_cols = 256

    @pl.loop(0, half // tile_cols)
    def _(tile):
        first = pl.multiple_of(tile * tile_cols, tile_cols)
        pre = []
        for base in (0, half):
            cols = pl.ds(base + first, tile_cols)
            pre.append(
                jnp.dot(normed[:rows, :half], glu_all[0, :, cols], preferred_element_type=jnp.float32)
                + jnp.dot(normed[:rows, half:], glu_all[1, :, cols], preferred_element_type=jnp.float32)
            )
        gated = jnp.where(live, pre[0] * jax.nn.sigmoid(pre[1]), 0.0).astype(jnp.bfloat16)
        cols = pl.ds(first, tile_cols)
        edge[0, :, cols] = gated[:HALO]
        edge[1, :, cols] = gated[rows - HALO :]
        padded[pl.ds(HALO, rows), cols] = gated.astype(jnp.float32)

    tail = start(copy("tail", edge.at[1], edge_in.at[0], "right"))
    head = start(copy("head", edge.at[0], edge_in.at[1], "left"))
    tail.wait_recv()
    head.wait_recv()
    has_left = jnp.where(f > 0, 1.0, 0.0)
    has_right = jnp.where(f < ring - 1, 1.0, 0.0)
    padded[:HALO, :] = edge_in[0].astype(jnp.float32) * has_left
    padded[HALO + rows :, :] = edge_in[1].astype(jnp.float32) * has_right

    lanes = 128
    step_rows = 64

    @pl.loop(0, half // lanes)
    def _(tile):
        cols = pl.ds(pl.multiple_of(tile * lanes, lanes), lanes)
        taps = taps_ref[:, cols].astype(jnp.float32)
        for first in range(0, rows, step_rows):
            depth = jnp.zeros((step_rows, lanes), jnp.float32)
            for tap in range(KERNEL):
                at_row = first + tap + HALO - KERNEL // 2
                depth = depth + padded[at_row : at_row + step_rows, cols] * taps[tap : tap + 1]
            hidden[first : first + step_rows, cols] = (depth * jax.nn.sigmoid(depth)).astype(jnp.bfloat16)

    here[3].wait()
    wide["pw", "y", 0].wait_recv()
    wide["pw", "y", 1].wait_recv()
    conv[1] = jnp.dot(
        hidden[...], pw_all[1 - h], preferred_element_type=jnp.float32
    ).astype(jnp.bfloat16)
    given = start(copy("conv", conv.at[1], conv_in, "core"))
    conv[0] = jnp.dot(
        hidden[...], pw_all[h], preferred_element_type=jnp.float32
    ).astype(jnp.bfloat16)
    given.wait_recv()
    both = (conv[0].astype(jnp.float32) + conv_in[...].astype(jnp.float32)).astype(jnp.bfloat16)
    out_ref[...] = (stream[h].astype(jnp.float32) + both.astype(jnp.float32)).astype(jnp.bfloat16)
    for c in started:
        c.wait_send()


def fused(frames_in, lengths, w_query, w_key, w_value, w_out, w_glu, dw_kernel, w_pw):
    rows, half = frames_in.shape[1:]
    att = w_query.shape[1]
    width = 2 * half
    ring = lax.axis_size("frames")
    shard = jnp.concatenate([w_query, w_key, w_value, w_out.T], axis=1)
    glu = w_glu.reshape(w_glu.shape[0], 2 * w_glu.shape[2])
    bf16, f32 = jnp.bfloat16, jnp.float32
    vmem = pl.BlockSpec(memory_space=pltpu.VMEM)
    anywhere = pl.BlockSpec(memory_space=pl.ANY)
    copies = 48
    result = pl.pallas_call(
        block_kernel,
        out_shape=jax.ShapeDtypeStruct((rows, half), bf16),
        in_specs=[anywhere, pl.BlockSpec(memory_space=pltpu.SMEM), anywhere, anywhere, vmem, anywhere],
        out_specs=vmem,
        scratch_shapes=[
            pltpu.VMEM((2, ring * rows, half), bf16),
            pltpu.VMEM((width, 4 * att), bf16),
            pltpu.VMEM((2,) + glu.shape, bf16),
            pltpu.VMEM((2,) + w_pw.shape, bf16),
            pltpu.VMEM((ring * rows, width), bf16),
            pltpu.VMEM((rows, att), bf16),
            pltpu.VMEM((2, ring * rows, att), bf16),
            pltpu.VMEM((rows, att), bf16),
            pltpu.VMEM((2, rows, half), bf16),
            pltpu.VMEM((2, rows, half), bf16),
            pltpu.VMEM((2, rows, half), bf16),
            pltpu.VMEM((rows + 2 * HALO, half), f32),
            pltpu.VMEM((2, HALO, half), bf16),
            pltpu.VMEM((2, HALO, half), bf16),
            pltpu.VMEM((rows, half), bf16),
            pltpu.VMEM((2, rows, half), bf16),
            pltpu.VMEM((rows, half), bf16),
            pltpu.SemaphoreType.DMA((4,)),
            pltpu.SemaphoreType.DMA((copies,)),
            pltpu.SemaphoreType.DMA((copies,)),
        ],
        compiler_params=pltpu.CompilerParams(
            collective_id=0, has_side_effects=True, vmem_limit_bytes=52 * 2**20
        ),
        cost_estimate=pl.CostEstimate(
            flops=2 * rows * width * (3 * att + 4 * half), bytes_accessed=2 * width * (4 * att + 6 * half),
            transcendentals=rows * rows * ring * 4,
        ),
    )(frames_in[0], lengths, shard, glu, dw_kernel, w_pw)
    return result[None]


def fits(mesh):
    sizes = dict(mesh.shape)
    return sizes["groups"] == 2 and sizes["fsdp"] == 2 and sizes["heads"] == 2 and sizes["frames"] == 4


def solution(mesh):
    in_specs = (
        P(("groups", "fsdp"), "frames", "heads"),
        P(("groups", "fsdp")),
        P(("frames", "fsdp"), "heads"),
        P(("frames", "fsdp"), "heads"),
        P(("frames", "fsdp"), "heads"),
        P("heads", ("frames", "fsdp")),
        P("fsdp", None, "heads"),
        P(None, "heads"),
        P("heads", "fsdp"),
    )
    out_specs = P(("groups", "fsdp"), "frames", "heads")
    body = fused if fits(mesh) else shards
    return jax.shard_map(body, mesh=mesh, in_specs=in_specs, out_specs=out_specs, check_vma=False)
```
